512 devices in a mesh: slab: 16 (over x, z_lo), tile: 32 (over z_hi, y, core).
Axes of the slice: x: 4, y: 4, z: 16 (z_hi: 4, z_lo: 4; z = z_hi * 4 + z_lo), core: 2. Of those that a mesh axis runs over, the one named last changes fastest.
Arguments:
- positions: float32 [32, 32, 3, 128], P('slab', 'tile'), may hold values from 0 to 32, as said below
- species: int32 [32, 32, 128], P('slab', 'tile'), may hold values from 0 to 5
- occupied: int32 [32, 32, 128], P('slab', 'tile'), may hold values 0 or 1
- embedding: bfloat16 [6, 128], replicated, may hold values from -6 to 6
- first_radial_weight: float32 [2, 8, 128], replicated, may hold values from -2 to 2
- radial_two: float32 [2, 8, 128], replicated, may hold values from -2 to 2
- mix_scalar: bfloat16 [128, 128], replicated, may hold values from -0.5 to 0.5
- vector_channel_weight: bfloat16 [128, 128], replicated, may hold values from -0.5 to 0.5
- out_weight: bfloat16 [128, 128], replicated, may hold values from -0.5 to 0.5
- read_weight: float32 [128], replicated, may hold values from -0.5 to 0.5
Outputs:
- energies: float32 [32, 32, 128], P('slab', 'tile')
- forces: float32 [32, 32, 3, 128], P('slab', 'tile')
The draws below stay inside these ranges and needn't reach their ends.
Inputs may be any that keep to these rules, and one draw needn't show every extreme that they name: `positions`: coordinates in angstrom from the corner of the atom's own cell, which spans 5 along slab, 10 along tile and 32 along the third direction.
All inputs are finite; a program needn't handle non-finite values. No bound on the sum of `occupied` on one device may be relied on, other than what follows from the above.
Results may differ from the reference program's by a relative error of at most 0.023.
Values may be sent and summed in bfloat16 or wider, within the bound.
No kernel may reach another device: no remote copies, remote signals or barrier semaphores. Data moves between devices by JAX's collectives and lax.ppermute only.
A program may use at most 64 MiB of HBM per device.

```python
import jax
import jax.numpy as jnp
import numpy as np
from jax import lax

CHANNELS = 128
RADIAL = 8
SPECIES = 6
BLOCK = 128
CELL_ROWS = 32
TILES = 32


def draw_positions(key, part):
    key = jax.random.fold_in(key, 11)
    fraction = jax.random.uniform(key, (CELL_ROWS, TILES, 3, BLOCK), jnp.float32)
    extents = jnp.array([5.0, 10.0, BLOCK / 4.0], jnp.float32)
    return fraction * extents[None, None, :, None]


def plant(values, stream_key, least, top_value):
    dims = values.shape
    spot = [jax.random.randint(jax.random.fold_in(stream_key, axis), (), 0, dims[axis]) for axis in range(len(dims))]
    values = values.at[tuple(spot)].set(least)
    longest = dims.index(max(dims))
    spot[longest] = (spot[longest] + 1) % dims[longest]
    return values.at[tuple(spot)].set(top_value)


def centred(rng, dims, spread, bound, kind=jnp.bfloat16):
    drawn = jax.random.normal(rng, dims, jnp.float32) * spread
    return jnp.minimum(jnp.maximum(drawn, -bound), bound).astype(kind)


def setup_inputs(seed: int = 0) -> dict:
    streams_of = jax.random.split(jax.random.key(seed), 11)
    return {
        "positions": draw_positions(jax.random.fold_in(streams_of[10], 71), 0),
        "species": plant(jax.random.randint(streams_of[1], (CELL_ROWS, TILES, BLOCK), 0, SPECIES), jax.random.fold_in(streams_of[1], 1), 0, SPECIES - 1).astype(jnp.int32),
        "occupied": plant((jax.random.randint(streams_of[2], (CELL_ROWS, TILES, BLOCK), 0, 8) < 7).astype(jnp.int32), jax.random.fold_in(streams_of[2], 1), 0, 1),
        "embedding": centred(streams_of[3], (SPECIES, CHANNELS), 1.0, 6.0),
        "first_radial_weight": centred(streams_of[4], (2, RADIAL, CHANNELS), 0.35, 2.0, jnp.float32),
        "radial_two": centred(streams_of[5], (2, RADIAL, CHANNELS), 0.35, 2.0, jnp.float32),
        "mix_scalar": centred(streams_of[6], (CHANNELS, CHANNELS), CHANNELS ** -0.5, 0.5),
        "vector_channel_weight": centred(streams_of[7], (CHANNELS, CHANNELS), CHANNELS ** -0.5, 0.5),
        "out_weight": centred(streams_of[8], (CHANNELS, CHANNELS), CHANNELS ** -0.5, 0.5),
        "read_weight": centred(streams_of[9], (CHANNELS,), CHANNELS ** -0.5, 0.5, jnp.float32),
    }


CUTOFF = 5.0
CUTOFF_SQUARE = 25.0
CELL_SLAB = 5.0
CELL_TILE = 10.0
NEIGHBOUR_DIVISOR = 4.0
STEPS_AROUND = [(slab_step, tile_step) for slab_step in (-1, 0, 1) for tile_step in (-1, 0, 1)]
OWN_CELLS = np.array([4, 7], dtype=np.int32)
SOURCE_TABLE = np.array([[(own_row + 1 + pair[0]) * 3 + 1 + pair[1] for pair in STEPS_AROUND] for own_row in (0, 1)], dtype=np.int32)
SHIFT_TABLE = np.array([[[pair[0] * CELL_SLAB, pair[1] * CELL_TILE, 0.0] for pair in STEPS_AROUND] for own_row in (0, 1)], dtype=np.float32)
SELF_TABLE = np.array([[int(pair[0] == 0 and pair[1] == 0) for pair in STEPS_AROUND] for own_row in (0, 1)], dtype=np.int32)

def widened(values):
    return lax.optimization_barrier(values).astype(jnp.float32)

def edge_kernels(receivers, senders, receiver_codes, sender_codes, same_block, basis_count):
    offsets = senders[:, None, :] - receivers[:, :, None]
    scaled = lax.optimization_barrier(jnp.sum(offsets * offsets, axis=0)) / CUTOFF_SQUARE
    length = receivers.shape[1]
    row_ids = lax.broadcasted_iota(jnp.int32, (length, length), 0)
    col_ids = lax.broadcasted_iota(jnp.int32, (length, length), 1)
    distinct = jnp.logical_or(jnp.logical_not(same_block), row_ids != col_ids)
    present = distinct & (receiver_codes[:, None] > -0.5) & (sender_codes[None, :] > -0.5)
    envelope = jnp.where(present, jnp.square(jnp.maximum(1.0 - scaled, 0.0)), 0.0)
    centres = (jnp.arange(basis_count, dtype=jnp.float32) + 0.5) / basis_count
    radial = jnp.exp(-0.5 * jnp.square((scaled[None] - centres[:, None, None]) * basis_count)) * envelope[None]
    directed = radial[:, None] * (offsets / CUTOFF)[None]
    return jnp.concatenate([radial[:, None], directed], axis=1).astype(jnp.bfloat16)

def pair_lists(block_index):
    sources = jnp.asarray(SOURCE_TABLE)[block_index]
    shifts = jnp.asarray(SHIFT_TABLE)[block_index]
    selves = jnp.asarray(SELF_TABLE)[block_index]
    return (sources, shifts, selves)

def first_layer(ext_positions, ext_codes, embedding, first_radial_weight, mix_scalar, vector_channel_weight):
    basis_count = first_radial_weight.shape[1]
    species_count = embedding.shape[0]
    length = ext_positions.shape[2]
    labels = jnp.arange(species_count, dtype=jnp.float32)
    species_hot = (jnp.abs(ext_codes[:, None, :] - labels[None, :, None]) < 0.5).astype(jnp.bfloat16)
    element_lookup = embedding.astype(jnp.float32)
    own_table = jnp.asarray(OWN_CELLS)

    def block_update(block_index):
        own_index = own_table[block_index]
        receivers = lax.dynamic_index_in_dim(ext_positions, own_index, 0, False)
        receiver_codes = lax.dynamic_index_in_dim(ext_codes, own_index, 0, False)

        def visit_pair(running_totals, listed):
            source, shift, itself = listed
            senders = lax.dynamic_index_in_dim(ext_positions, source, 0, False) + shift[:, None]
            sender_codes = lax.dynamic_index_in_dim(ext_codes, source, 0, False)
            sender_onehot = lax.dynamic_index_in_dim(species_hot, source, 0, False)
            radial_filters = widened(edge_kernels(receivers, senders, receiver_codes, sender_codes, itself > 0, basis_count))
            tallied_entries = jnp.einsum('uxfy,zy->uxfz', radial_filters, sender_onehot.astype(jnp.float32))
            return (running_totals + tallied_entries, None)
        start_totals = jnp.zeros((basis_count, 4, length, species_count), jnp.float32)
        running_totals, ignored = lax.scan(jax.checkpoint(visit_pair), start_totals, pair_lists(block_index))
        fetched_rows = jnp.einsum('gpen,nw->gpwe', running_totals, element_lookup)
        scalar_sum = jnp.einsum('bc,bci->ci', first_radial_weight[0], fetched_rows[:, 0]) / NEIGHBOUR_DIVISOR
        pooled_vector = jnp.einsum('kt,kwtx->wtx', first_radial_weight[1], fetched_rows[:, 1:]) / NEIGHBOUR_DIVISOR
        own_hot = lax.dynamic_index_in_dim(species_hot, own_index, 0, False)
        initial = jnp.dot(embedding.T, own_hot, preferred_element_type=jnp.float32)
        invariant = (scalar_sum + lax.optimization_barrier(jnp.sum(pooled_vector * pooled_vector, axis=0))).astype(jnp.bfloat16)
        hidden = jnp.dot(mix_scalar.T, invariant, preferred_element_type=jnp.float32)
        incoming_vector = pooled_vector.astype(jnp.bfloat16)
        new_vector = jnp.stack([jnp.dot(vector_channel_weight.T, incoming_vector[axis_index], preferred_element_type=jnp.float32) for axis_index in range(3)])
        return (initial + jax.nn.silu(hidden), new_vector)
    return lax.map(block_update, jnp.arange(2, dtype=jnp.int32))

def second_layer(ext_positions, ext_codes, ext_features, radial_two, out_weight, read_weight):
    basis_count = radial_two.shape[1]
    width = out_weight.shape[0]
    length = ext_positions.shape[2]
    own_table = jnp.asarray(OWN_CELLS)

    def block_energy(block_index):
        own_index = own_table[block_index]
        receivers = lax.dynamic_index_in_dim(ext_positions, own_index, 0, False)
        receiver_codes = lax.dynamic_index_in_dim(ext_codes, own_index, 0, False)

        def visit_pair(running_totals, listed):
            source, shift, itself = listed
            senders = lax.dynamic_index_in_dim(ext_positions, source, 0, False) + shift[:, None]
            sender_codes = lax.dynamic_index_in_dim(ext_codes, source, 0, False)
            sender_features = widened(lax.dynamic_index_in_dim(ext_features, source, 0, False).astype(jnp.bfloat16))
            scalars = sender_features[:width]
            vectors = sender_features[width:].reshape((3, width, length))
            radial_filters = widened(edge_kernels(receivers, senders, receiver_codes, sender_codes, itself > 0, basis_count))
            first_term = jnp.einsum('bij,cj->bci', radial_filters[:, 0], scalars)
            second_term = jnp.einsum('bdij,dcj->bci', radial_filters[:, 1:], vectors)
            return ((running_totals[0] + first_term, running_totals[1] + second_term), None)
        empty_sum = jnp.zeros((basis_count, width, length), jnp.float32)
        sums, ignored = lax.scan(jax.checkpoint(visit_pair), (empty_sum, empty_sum), pair_lists(block_index))
        message = (jnp.einsum('bc,bci->ci', radial_two[0], sums[0]) + jnp.einsum('bc,bci->ci', radial_two[1], sums[1])) / NEIGHBOUR_DIVISOR
        own_scalar = lax.dynamic_index_in_dim(ext_features, own_index, 0, False)[:width]
        combined = (own_scalar + message).astype(jnp.bfloat16)
        hidden = jnp.dot(out_weight.T, combined, preferred_element_type=jnp.float32)
        present = (receiver_codes > -0.5).astype(jnp.float32)
        return present * lax.optimization_barrier(jnp.sum(read_weight[:, None] * jax.nn.silu(hidden), axis=0))
    return lax.map(block_energy, jnp.arange(2, dtype=jnp.int32))

def padded_grid(grid):
    return jnp.pad(grid, ((1, 1), (1, 1)) + ((0, 0),) * (grid.ndim - 2), mode='wrap')

def window_starts(slab_index, tile_index, extra):
    anchor = jnp.zeros((), jnp.int32)
    return (slab_index * 2, tile_index) + (anchor,) * extra

def device_window(padded, slab_index, tile_index):
    starts = window_starts(slab_index, tile_index, padded.ndim - 2)
    window = lax.dynamic_slice(padded, starts, (4, 3) + padded.shape[2:])
    return window.reshape((12,) + padded.shape[2:])

def add_window(total, slab_index, tile_index, values):
    shaped = values.reshape((4, 3) + values.shape[1:])
    starts = window_starts(slab_index, tile_index, total.ndim - 2)
    current = lax.dynamic_slice(total, starts, shaped.shape)
    return lax.dynamic_update_slice(total, current + shaped, starts)

def fold_grid(padded):
    rows = padded[1:-1]
    rows = rows.at[0].add(padded[-1]).at[-1].add(padded[0])
    core = rows[:, 1:-1]
    return core.at[:, 0].add(rows[:, -1]).at[:, -1].add(rows[:, 0])

def reference(positions, species, occupied, embedding, first_radial_weight, radial_two, mix_scalar, vector_channel_weight, out_weight, read_weight):
    row_count = positions.shape[0]
    tile_count = positions.shape[1]
    length = positions.shape[3]
    slab_count = row_count // 2
    width = embedding.shape[1]
    devices = slab_count * tile_count
    codes = jnp.where(occupied > 0, species, -1).astype(jnp.float32)
    packet = jnp.concatenate([positions, codes[:, :, None]], axis=2)
    packet_padded = padded_grid(packet)
    device_ids = jnp.arange(devices, dtype=jnp.int32)

    def locate(device):
        return (device // tile_count, device % tile_count)

    def extended(device):
        slab_index, tile_index = locate(device)
        window = device_window(packet_padded, slab_index, tile_index)
        return (window[:, :3], window[:, 3])

    def layer_one(device):
        ext_positions, ext_codes = extended(device)
        scalar_part, vector_part = first_layer(ext_positions, ext_codes, embedding, first_radial_weight, mix_scalar, vector_channel_weight)
        joined = jnp.concatenate([scalar_part[:, None], vector_part], axis=1).astype(jnp.bfloat16)
        return joined.reshape((2, 4 * width, length))
    features = lax.map(layer_one, device_ids)
    features = features.reshape((slab_count, tile_count, 2, 4 * width, length)).transpose((0, 2, 1, 3, 4))
    features = features.reshape((row_count, tile_count, 4 * width, length))
    feature_padded = padded_grid(features)

    def layer_two(carry, device):
        feature_acc, position_acc = carry
        slab_index, tile_index = locate(device)
        ext_positions, ext_codes = extended(device)
        ext_features = device_window(feature_padded, slab_index, tile_index).astype(jnp.float32)
        energies, pullback = jax.vjp(lambda moved_atoms, carried: second_layer(moved_atoms, ext_codes, carried, radial_two, out_weight, read_weight), ext_positions, ext_features)
        position_grad, feature_grad = pullback(jnp.ones_like(energies))
        feature_acc = add_window(feature_acc, slab_index, tile_index, feature_grad)
        position_acc = add_window(position_acc, slab_index, tile_index, position_grad)
        return ((feature_acc, position_acc), energies)
    feature_start = jnp.zeros(feature_padded.shape, jnp.float32)
    position_start = jnp.zeros(packet_padded.shape[:2] + (3, length), jnp.float32)
    carried, energies = lax.scan(layer_two, (feature_start, position_start), device_ids)
    feature_acc, position_acc = carried
    feature_total = widened(fold_grid(feature_acc).astype(jnp.bfloat16))

    def layer_one_back(position_acc, device):
        slab_index, tile_index = locate(device)
        ext_positions, ext_codes = extended(device)
        anchor = jnp.zeros((), jnp.int32)
        own_grad = lax.dynamic_slice(feature_total, (slab_index * 2, tile_index, anchor, anchor), (2, 1, 4 * width, length))[:, 0]
        scalar_grad = own_grad[:, :width]
        vector_grad = own_grad[:, width:].reshape((2, 3, width, length))
        ignored, pullback = jax.vjp(lambda moved_atoms: first_layer(moved_atoms, ext_codes, embedding, first_radial_weight, mix_scalar, vector_channel_weight), ext_positions)
        position_grad = pullback((scalar_grad, vector_grad))[0]
        return (add_window(position_acc, slab_index, tile_index, position_grad), None)
    position_acc, ignored = lax.scan(layer_one_back, position_acc, device_ids)
    forces = -fold_grid(position_acc)
    energies = energies.reshape((slab_count, tile_count, 2, length)).transpose((0, 2, 1, 3))
    return (energies.reshape((row_count, tile_count, length)), forces)
```

```python
import jax
import jax.numpy as jnp
import numpy as np
from jax import lax
from jax.experimental import pallas as pl
from jax.experimental.pallas import tpu as pltpu
from jax.sharding import PartitionSpec as P

F32 = jnp.float32
BF16 = jnp.bfloat16
LENGTH = 128
BASIS = 8
NEAR = 9
FAR = 1000.0
INV_CUTOFF = 0.2
CELL_SLAB = 5.0
CELL_TILE = 10.0
VMEM_LIMIT = 56 * 1024 * 1024
FOLD = np.exp(-0.5 * np.arange(BASIS) * (np.arange(BASIS) + 1)).astype(np.float32)


def silu_pair(value):
    gate = 1.0 / (1.0 + jnp.exp(-value))
    return value * gate, gate * (1.0 + value * (1.0 - gate))


def place_atoms(pos_refs, send_ref, recv_ref):
    for tile, ref in enumerate(pos_refs):
        for row in range(4):
            real = ref[row, 3:4, :] > -0.5
            shift = ((row - 1) * CELL_SLAB, (tile - 1) * CELL_TILE, 0.0)
            for d in range(3):
                coords = ref[row, d : d + 1, :]
                sender = jnp.where(real, coords + shift[d], -FAR) * INV_CUTOFF
                send_ref[row * 3 + tile, d : d + 1, :] = sender
                if tile == 1 and row in (1, 2):
                    receiver = jnp.where(real, coords + shift[d], FAR) * INV_CUTOFF
                    spread = jnp.broadcast_to(receiver, (LENGTH, LENGTH))
                    recv_ref[row - 1, d] = jnp.transpose(spread)


def species_column(code_row):
    return jnp.transpose(jnp.broadcast_to(code_row, (LENGTH, LENGTH)))


def species_hot(code_row):
    lanes = lax.broadcasted_iota(jnp.int32, (LENGTH, LENGTH), 1)
    species = (lanes & 7).astype(F32)
    return jnp.where(species_column(code_row) == species, 1.0, 0.0).astype(BF16)


def pair_geometry(send_ref, recv_ref, block, cell, first, rows):
    apart = [
        send_ref[cell, d : d + 1, :] - recv_ref[block, d, pl.ds(first, rows), :] for d in range(3)
    ]
    square = apart[0] * apart[0] + apart[1] * apart[1] + apart[2] * apart[2]
    square = jnp.minimum(square, 1.0)
    eight = 8.0 * square
    centred = eight - 0.5
    return apart, eight, centred, jnp.exp(-0.5 * centred * centred), jnp.exp(eight), 1.0 - square


def fill_kernels(send_ref, recv_ref, kern_ref, block):
    rows = 16

    def body(step, carry):
        first = pl.multiple_of(step * rows, rows)
        for tile in range(3):
            for near in range(3):
                cell = (block + near) * 3 + tile
                apart, _, _, gauss, ratio, rest = pair_geometry(
                    send_ref, recv_ref, block, cell, first, rows
                )
                value = gauss * (rest * rest)
                if tile == 1 and near == 1:
                    own = first + lax.broadcasted_iota(jnp.int32, (rows, LENGTH), 0)
                    other = lax.broadcasted_iota(jnp.int32, (rows, LENGTH), 1)
                    value = jnp.where(own == other, 0.0, value)
                narrow = [a.astype(BF16) for a in apart]
                column = (tile * 3 + near) * LENGTH
                for b in range(BASIS):
                    radial = value.astype(BF16)
                    kern_ref[pl.ds(b * LENGTH + first, rows), column : column + LENGTH] = radial
                    for d in range(3):
                        at = (d + 1) * BASIS * LENGTH + b * LENGTH
                        kern_ref[pl.ds(at + first, rows), column : column + LENGTH] = (
                            radial * narrow[d]
                        )
                    if b + 1 < BASIS:
                        value = value * ratio
        return carry

    lax.fori_loop(0, LENGTH // rows, body, 0)


def weighted_sum(kern_ref, part, rhs, weights):
    depth = BASIS * LENGTH
    product = jnp.dot(
        kern_ref[part * depth : (part + 1) * depth, :], rhs, preferred_element_type=F32
    )
    total = product[:LENGTH] * weights[0:1, :]
    for b in range(1, BASIS):
        total = total + product[b * LENGTH : (b + 1) * LENGTH] * weights[b : b + 1, :]
    return total


def nearby(refs, block, lo, width):
    return jnp.concatenate(
        [refs[tile][block + near, lo : lo + width, :] for tile in range(3) for near in range(3)],
        axis=0,
    )


def first_kernel(
    left, middle, right, table, weights, mix, mixv, feat_out, hidden_out, vector_out,
    send_ref, recv_ref, kern_ref, start_ref,
):
    pos_refs = (left, middle, right)
    place_atoms(pos_refs, send_ref, recv_ref)
    for tile in range(3):
        for row in range(4):
            hot = species_hot(pos_refs[tile][row, 3:4, :])
            start_ref[tile, row] = jnp.dot(hot, table[...], preferred_element_type=F32).astype(BF16)

    def body(block, carry):
        fill_kernels(send_ref, recv_ref, kern_ref, block)
        rhs = jnp.concatenate(
            [start_ref[tile, block + near] for tile in range(3) for near in range(3)], axis=0
        )
        scalar = weighted_sum(kern_ref, 0, rhs, weights[0])
        invariant = scalar
        for d in range(3):
            vector = weighted_sum(kern_ref, d + 1, rhs, weights[1])
            vector_out[block, d] = vector
            invariant = invariant + vector * vector
            mixed = jnp.dot(vector.astype(BF16), mixv[...], preferred_element_type=F32)
            feat_out[block, (d + 1) * LENGTH : (d + 2) * LENGTH, :] = mixed.astype(BF16)
        hidden = jnp.dot(invariant.astype(BF16), mix[...], preferred_element_type=F32)
        hidden_out[block] = hidden
        start = start_ref[1, block + 1].astype(F32)
        feat_out[block, :LENGTH, :] = (start + silu_pair(hidden)[0]).astype(BF16)
        return carry

    lax.fori_loop(0, 2, body, 0)


def second_kernel(
    left, middle, right, feat_left, feat_middle, feat_right, weights, out_weight, out_turned, read,
    energy_out, pull_out, send_ref, recv_ref, kern_ref,
):
    pos_refs = (left, middle, right)
    feats = (feat_left, feat_middle, feat_right)
    place_atoms(pos_refs, send_ref, recv_ref)

    def body(block, carry):
        fill_kernels(send_ref, recv_ref, kern_ref, block)
        message = weighted_sum(kern_ref, 0, nearby(feats, block, 0, LENGTH), weights[0])
        for d in range(3):
            rhs = nearby(feats, block, (d + 1) * LENGTH, LENGTH)
            message = message + weighted_sum(kern_ref, d + 1, rhs, weights[1])
        own = feat_middle[block + 1, :LENGTH, :].astype(F32)
        combined = (own + message).astype(BF16)
        hidden = jnp.dot(combined, out_weight[...], preferred_element_type=F32)
        value, slope = silu_pair(hidden)
        present = species_column(middle[block + 1, 3:4, :]) > -0.5
        energy = jnp.where(present, jnp.sum(value * read[...], axis=1, keepdims=True), 0.0)
        energy_out[block] = jnp.transpose(jnp.broadcast_to(energy, (LENGTH, LENGTH)))[:8]
        back = jnp.where(present, slope * read[...], 0.0).astype(BF16)
        pull = jnp.dot(back, out_turned[...], preferred_element_type=F32)
        pull_out[block] = pull.astype(BF16)
        return carry

    lax.fori_loop(0, 2, body, 0)


def third_kernel(
    left, middle, right, feat_left, feat_middle, feat_right, pull_left, pull_middle, pull_right,
    hidden, vectors, weights_two, mix_turned, mixv_turned, spread, force_out,
    send_ref, recv_ref, kern_ref, hot_ref, lhs_ref, deriv_ref, row_ref,
):
    pos_refs = (left, middle, right)
    feats = (feat_left, feat_middle, feat_right)
    pulls = (pull_left, pull_middle, pull_right)
    place_atoms(pos_refs, send_ref, recv_ref)
    for tile in range(3):
        for row in range(4):
            hot_ref[tile, row] = species_hot(pos_refs[tile][row, 3:4, :])
    force_out[...] = jnp.zeros(force_out.shape, F32)
    depth = BASIS * LENGTH

    def body(block, carry):
        fill_kernels(send_ref, recv_ref, kern_ref, block)
        rhs = nearby(pulls, block, 0, LENGTH)
        pull = pull_middle[block + 1].astype(F32)
        scalar_grad = pull + weighted_sum(kern_ref, 0, rhs, weights_two[0])
        scalar_grad = scalar_grad.astype(BF16).astype(F32)
        hidden_grad = (scalar_grad * silu_pair(hidden[block])[1]).astype(BF16)
        inv_grad = jnp.dot(hidden_grad, mix_turned[...], preferred_element_type=F32)
        inv_grad = inv_grad.astype(BF16).astype(F32)
        grads = [inv_grad]
        for d in range(3):
            vector_grad = -weighted_sum(kern_ref, d + 1, rhs, weights_two[1])
            passed = jnp.dot(
                vector_grad.astype(BF16), mixv_turned[...], preferred_element_type=F32
            )
            passed = passed.astype(BF16).astype(F32)
            grads.append(passed + 2.0 * vectors[block, d] * inv_grad)
        lane_basis = lax.broadcasted_iota(jnp.int32, (LENGTH, LENGTH), 1) >> 3
        for r in range(4):
            which = min(r, 1)
            table_grad = jnp.dot(
                grads[r],
                spread[which],
                preferred_element_type=F32,
                precision=lax.Precision.HIGHEST,
            )
            for b in range(BASIS):
                at = r * depth + b * LENGTH
                scaled = pull * weights_two[which, b : b + 1, :]
                lhs_ref[at : at + LENGTH, :LENGTH] = scaled.astype(BF16)
                lhs_ref[at : at + LENGTH, LENGTH:] = jnp.where(
                    lane_basis == b, table_grad, 0.0
                ).astype(BF16)
        row_ref[...] = jnp.zeros(row_ref.shape, F32)
        rows = 16
        for tile in range(3):
            for near in range(3):
                for r in range(4):
                    sender = jnp.concatenate(
                        [
                            feats[tile][block + near, r * LENGTH : (r + 1) * LENGTH, :],
                            hot_ref[tile, block + near],
                        ],
                        axis=1,
                    )
                    deriv_ref[r * depth : (r + 1) * depth, :] = lax.dot_general(
                        lhs_ref[r * depth : (r + 1) * depth, :],
                        sender,
                        (((1,), (1,)), ((), ())),
                        preferred_element_type=F32,
                    )
                cell = (block + near) * 3 + tile

                def chain(step, columns):
                    first = pl.multiple_of(step * rows, rows)
                    apart, eight, centred, gauss, ratio, rest = pair_geometry(
                        send_ref, recv_ref, block, cell, first, rows
                    )
                    if tile == 1 and near == 1:
                        own = first + lax.broadcasted_iota(jnp.int32, (rows, LENGTH), 0)
                        other = lax.broadcasted_iota(jnp.int32, (rows, LENGTH), 1)
                        rest = jnp.where(own == other, 0.0, rest)
                    along = [None, None, None]
                    value = None
                    slope = None
                    for b in range(BASIS - 1, -1, -1):
                        parts = [
                            deriv_ref[pl.ds(r * depth + b * LENGTH + first, rows), :]
                            for r in range(4)
                        ]
                        joint = parts[0]
                        for d in range(3):
                            joint = joint + apart[d] * parts[d + 1]
                            along[d] = (
                                parts[d + 1]
                                if along[d] is None
                                else along[d] * ratio + parts[d + 1]
                            )
                        if value is None:
                            value = joint
                        else:
                            slope = value if slope is None else slope * ratio + value
                            value = value * ratio + joint
                    slope = slope * ratio
                    scale = gauss * rest
                    radial = (
                        scale * (8.0 * rest * (slope - centred * value) - 2.0 * value)
                    ) * (2.0 * INV_CUTOFF)
                    envelope = scale * rest * INV_CUTOFF
                    out = []
                    for d in range(3):
                        pushed = envelope * along[d] + radial * apart[d]
                        row_ref[d, pl.ds(first, rows), :] = (
                            row_ref[d, pl.ds(first, rows), :] + pushed
                        )
                        out.append(columns[d] + pushed)
                    return tuple(out)

                zero = jnp.zeros((rows, LENGTH), F32)
                columns = lax.fori_loop(0, LENGTH // rows, chain, (zero, zero, zero))
                for d in range(3):
                    force_out[tile, block + near, d : d + 1, :] = force_out[
                        tile, block + near, d : d + 1, :
                    ] - jnp.sum(columns[d], axis=0, keepdims=True)
        for d in range(3):
            total = jnp.sum(jnp.transpose(row_ref[d]), axis=0, keepdims=True)
            force_out[1, block + 1, d : d + 1, :] = (
                force_out[1, block + 1, d : d + 1, :] + total
            )
        return carry

    lax.fori_loop(0, 2, body, 0)


def ring(block, axis, step):
    count = lax.axis_size(axis)
    return lax.ppermute(block, axis, [(i, (i + step) % count) for i in range(count)])


def gather_near(cells):
    above = ring(cells[1:], "slab", 1)
    below = ring(cells[:1], "slab", -1)
    column = jnp.concatenate([above, cells, below], axis=0)
    return ring(column, "tile", 1), column, ring(column, "tile", -1)


def send_home(parts):
    column = parts[1] + ring(parts[0], "tile", -1) + ring(parts[2], "tile", 1)
    from_next = ring(column[:1], "slab", -1)
    from_last = ring(column[3:], "slab", 1)
    return column[1:3] + jnp.concatenate([from_last, from_next], axis=0)


def kernel_call(body, outs, scratch, flops):
    return pl.pallas_call(
        body,
        out_shape=[jax.ShapeDtypeStruct(shape, kind) for shape, kind in outs],
        scratch_shapes=[pltpu.VMEM(shape, kind) for shape, kind in scratch],
        compiler_params=pltpu.CompilerParams(vmem_limit_bytes=VMEM_LIMIT),
        cost_estimate=pl.CostEstimate(flops=flops, bytes_accessed=1 << 20, transcendentals=0),
    )


def on_device(
    positions, species, occupied, embedding, first_radial_weight, radial_two, mix_scalar,
    vector_channel_weight, out_weight, read_weight,
):
    codes = jnp.where(occupied > 0, species, -1).astype(F32)
    packet = jnp.concatenate([positions, codes[:, :, None]], axis=2)[:, 0]
    fold = jnp.asarray(FOLD)[None, :, None] * 0.25
    weights_one = first_radial_weight * fold
    weights_two = radial_two * fold
    table = jnp.zeros((LENGTH, LENGTH), BF16).at[: embedding.shape[0]].set(embedding)
    padded = jnp.pad(embedding.astype(F32), ((0, 8 - embedding.shape[0]), (0, 0)))
    spread = weights_one[:, :, None, :] * padded[None, None]
    spread = spread.reshape((2, 64, LENGTH))
    spread = jnp.pad(spread, ((0, 0), (0, 64), (0, 0))).transpose((0, 2, 1))
    read = read_weight[None, :]

    places = gather_near(packet)
    geometry = [
        ((12, 3, LENGTH), F32),
        ((2, 3, LENGTH, LENGTH), F32),
        ((4 * BASIS * LENGTH, NEAR * LENGTH), BF16),
    ]
    features, hidden, vectors = kernel_call(
        first_kernel,
        [
            ((2, 4 * LENGTH, LENGTH), BF16),
            ((2, LENGTH, LENGTH), F32),
            ((2, 3, LENGTH, LENGTH), F32),
        ],
        geometry + [((3, 4, LENGTH, LENGTH), BF16)],
        2400000000,
    )(*places, table, weights_one, mix_scalar, vector_channel_weight)
    all_features = gather_near(features)
    energies, pull = kernel_call(
        second_kernel,
        [((2, 8, LENGTH), F32), ((2, LENGTH, LENGTH), BF16)],
        geometry,
        2400000000,
    )(*places, *all_features, weights_two, out_weight, out_weight.T, read)
    all_pulls = gather_near(pull)
    (parts,) = kernel_call(
        third_kernel,
        [((3, 4, 3, LENGTH), F32)],
        geometry
        + [
            ((3, 4, LENGTH, LENGTH), BF16),
            ((4 * BASIS * LENGTH, 2 * LENGTH), BF16),
            ((4 * BASIS * LENGTH, LENGTH), F32),
            ((3, LENGTH, LENGTH), F32),
        ],
        7200000000,
    )(
        *places, *all_features, *all_pulls, hidden, vectors, weights_two, mix_scalar.T,
        vector_channel_weight.T, spread,
    )
    forces = send_home(parts)
    return energies[:, :1], forces[:, None]


def solution(mesh):
    in_specs = (
        P("slab", "tile", None, None),
        P("slab", "tile", None),
        P("slab", "tile", None),
        P(),
        P(),
        P(),
        P(),
        P(),
        P(),
        P(),
    )
    out_specs = (P("slab", "tile", None), P("slab", "tile", None, None))
    return jax.shard_map(
        on_device, mesh=mesh, in_specs=in_specs, out_specs=out_specs, check_vma=False
    )
```

```python
import functools

import jax
import jax.numpy as jnp
from jax import lax
from jax.experimental import pallas as pl
from jax.experimental.pallas import tpu as pltpu
from jax.sharding import PartitionSpec as P

F32 = jnp.float32
BF16 = jnp.bfloat16
LENGTH = 128
BASIS = 8
NEAR = 9
FAR = 1000.0
INV_CUTOFF = 0.2
CELL_SLAB = 5.0
CELL_TILE = 10.0
VMEM_LIMIT = 32 * 1024 * 1024


def silu_pair(value):
    gate = 1.0 / (1.0 + jnp.exp(-value))
    return value * gate, gate * (1.0 + value * (1.0 - gate))


OWN_SLOTS = ((0, 0), (1, 0), (2, 0))


def slots_of(flag_ref):
    flag = flag_ref[0]
    turn = (2 * flag - 1).astype(F32) * CELL_TILE
    return ((0, flag), (0, 1 - flag), (1, 1 - flag)), (turn, 0.0, -turn)


def place_atoms(pairs, slots, turns, send_ref, recv_ref):
    for tile in range(3):
        ref, member = pairs[slots[tile][0]], slots[tile][1]
        for row in range(4):
            cell = ref[member, row]
            real = cell[3:4] > -0.5
            shift = ((row - 1) * CELL_SLAB, turns[tile], 0.0)
            for d in range(3):
                coords = cell[d : d + 1] + shift[d]
                sender = jnp.where(real, coords, -FAR) * INV_CUTOFF
                send_ref[row * 3 + tile, d : d + 1, :] = sender
                if tile == 1 and row in (1, 2):
                    receiver = jnp.where(real, coords, FAR) * INV_CUTOFF
                    spread = jnp.broadcast_to(receiver, (LENGTH, LENGTH))
                    recv_ref[row - 1, d] = jnp.transpose(spread)


def folded(weights, which):
    order = lax.broadcasted_iota(jnp.int32, (BASIS, LENGTH), 0).astype(F32)
    return weights[which] * (0.25 * jnp.exp(-0.5 * order * (order + 1.0)))


def species_rows(embedding):
    table = embedding[...].astype(F32)
    return jnp.concatenate([table, jnp.zeros((8 - table.shape[0], LENGTH), F32)], axis=0)


def turned_dot(lhs, rhs, **kinds):
    return lax.dot_general(
        lhs, rhs, (((1,), (1,)), ((), ())), preferred_element_type=F32, **kinds
    )


def species_column(code_row):
    return jnp.transpose(jnp.broadcast_to(code_row, (LENGTH, LENGTH)))


def species_hot(code_row):
    lanes = lax.broadcasted_iota(jnp.int32, (LENGTH, LENGTH), 1)
    species = (lanes & 7).astype(F32)
    return jnp.where(species_column(code_row) == species, 1.0, 0.0).astype(BF16)


def pair_geometry(send_ref, recv_ref, block, cell, first, rows):
    apart = [
        send_ref[cell, d : d + 1, :] - recv_ref[block, d, pl.ds(first, rows), :] for d in range(3)
    ]
    square = apart[0] * apart[0] + apart[1] * apart[1] + apart[2] * apart[2]
    square = jnp.minimum(square, 1.0)
    eight = 8.0 * square
    centred = eight - 0.5
    return apart, eight, centred, jnp.exp(-0.5 * centred * centred), jnp.exp(eight), 1.0 - square


def fill_kernels(send_ref, recv_ref, kern_ref, block):
    rows = 16

    def body(step, carry):
        first = pl.multiple_of(step * rows, rows)
        for tile in range(3):
            for near in range(3):
                cell = (block + near) * 3 + tile
                apart, _, _, gauss, ratio, rest = pair_geometry(
                    send_ref, recv_ref, block, cell, first, rows
                )
                value = gauss * (rest * rest)
                if tile == 1 and near == 1:
                    own = first + lax.broadcasted_iota(jnp.int32, (rows, LENGTH), 0)
                    other = lax.broadcasted_iota(jnp.int32, (rows, LENGTH), 1)
                    value = jnp.where(own == other, 0.0, value)
                narrow = [a.astype(BF16) for a in apart]
                column = (tile * 3 + near) * LENGTH
                for b in range(BASIS):
                    radial = value.astype(BF16)
                    kern_ref[pl.ds(b * LENGTH + first, rows), column : column + LENGTH] = radial
                    for d in range(3):
                        at = (d + 1) * BASIS * LENGTH + b * LENGTH
                        kern_ref[pl.ds(at + first, rows), column : column + LENGTH] = (
                            radial * narrow[d]
                        )
                    if b + 1 < BASIS:
                        value = value * ratio
        return carry

    lax.fori_loop(0, LENGTH // rows, body, 0)


def weighted_sum(kern_ref, part, rhs, weights):
    depth = BASIS * LENGTH
    product = jnp.dot(
        kern_ref[part * depth : (part + 1) * depth, :], rhs, preferred_element_type=F32
    )
    total = product[:LENGTH] * weights[0:1, :]
    for b in range(1, BASIS):
        total = total + product[b * LENGTH : (b + 1) * LENGTH] * weights[b : b + 1, :]
    return total


def nearby(pairs, slots, block, lo, width):
    return jnp.concatenate(
        [
            pairs[which][member, block + near, lo : lo + width, :]
            for which, member in slots
            for near in range(3)
        ],
        axis=0,
    )


def first_kernel(
    flag, even, odd, embedding, weights, mix, mixv, feat_out, hidden_out, vector_out,
    send_ref, recv_ref, kern_ref, start_ref,
):
    pairs = (even, odd)
    slots, turns = slots_of(flag)
    place_atoms(pairs, slots, turns, send_ref, recv_ref)
    table = jnp.concatenate([species_rows(embedding)] * 16, axis=0).astype(BF16)
    for tile in range(3):
        for row in range(4):
            hot = species_hot(pairs[slots[tile][0]][slots[tile][1], row][3:4])
            start = jnp.dot(hot, table, preferred_element_type=F32) * 0.0625
            start_ref[tile, row] = start.astype(BF16)
    scale = [folded(weights, which) for which in range(2)]

    def body(block, carry):
        fill_kernels(send_ref, recv_ref, kern_ref, block)
        rhs = jnp.concatenate(
            [start_ref[tile, block + near] for tile in range(3) for near in range(3)], axis=0
        )
        scalar = weighted_sum(kern_ref, 0, rhs, scale[0])
        invariant = scalar
        for d in range(3):
            vector = weighted_sum(kern_ref, d + 1, rhs, scale[1])
            vector_out[block, d] = vector
            invariant = invariant + vector * vector
            mixed = jnp.dot(vector.astype(BF16), mixv[...], preferred_element_type=F32)
            feat_out[block, (d + 1) * LENGTH : (d + 2) * LENGTH, :] = mixed.astype(BF16)
        hidden = jnp.dot(invariant.astype(BF16), mix[...], preferred_element_type=F32)
        hidden_out[block] = hidden
        start = start_ref[1, block + 1].astype(F32)
        feat_out[block, :LENGTH, :] = (start + silu_pair(hidden)[0]).astype(BF16)
        return carry

    lax.fori_loop(0, 2, body, 0)


def second_kernel(
    flag, even, odd, feat_even, feat_mine, feat_odd, weights, out_weight, read, energy_out,
    pull_out, send_ref, recv_ref, kern_ref,
):
    slots, turns = slots_of(flag)
    feats = (feat_even, feat_mine, feat_odd)
    place_atoms((even, odd), slots, turns, send_ref, recv_ref)
    mine = slots[1][1]
    scale = [folded(weights, which) for which in range(2)]

    def body(block, carry):
        fill_kernels(send_ref, recv_ref, kern_ref, block)
        message = weighted_sum(kern_ref, 0, nearby(feats, OWN_SLOTS, block, 0, LENGTH), scale[0])
        for d in range(3):
            rhs = nearby(feats, OWN_SLOTS, block, (d + 1) * LENGTH, LENGTH)
            message = message + weighted_sum(kern_ref, d + 1, rhs, scale[1])
        own = feat_mine[0, block + 1, :LENGTH, :].astype(F32)
        combined = (own + message).astype(BF16)
        hidden = jnp.dot(combined, out_weight[...], preferred_element_type=F32)
        value, slope = silu_pair(hidden)
        present = species_column(even[mine, block + 1][3:4]) > -0.5
        energy = jnp.where(present, jnp.sum(value * read[...], axis=1, keepdims=True), 0.0)
        energy_out[block] = jnp.transpose(jnp.broadcast_to(energy, (LENGTH, LENGTH)))[:1]
        back = jnp.where(present, slope * read[...], 0.0).astype(BF16)
        pull_out[block] = turned_dot(back, out_weight[...]).astype(BF16)
        return carry

    lax.fori_loop(0, 2, body, 0)


def third_kernel(
    flag, even, odd, feat_even, feat_mine, feat_odd, pull_even, pull_odd, hidden, vectors,
    energies, embedding, weights_one, weights_two, mix, mixv, force_out,
    send_ref, recv_ref, kern_ref, hot_ref, lhs_ref, deriv_ref, row_ref,
):
    pairs = (even, odd)
    feats = (feat_even, feat_mine, feat_odd)
    pulls = (pull_even, pull_odd)
    slots, turns = slots_of(flag)
    mine = slots[1][1]
    place_atoms(pairs, slots, turns, send_ref, recv_ref)
    for tile in range(3):
        for row in range(4):
            hot_ref[tile, row] = species_hot(pairs[slots[tile][0]][slots[tile][1], row][3:4])
    scale_one = [folded(weights_one, which) for which in range(2)]
    scale_two = [folded(weights_two, which) for which in range(2)]
    table = species_rows(embedding)
    force_out[...] = jnp.zeros(force_out.shape, F32)
    depth = BASIS * LENGTH

    def body(block, carry):
        fill_kernels(send_ref, recv_ref, kern_ref, block)
        force_out[1, block + 1, 3:4, :] = energies[block]
        rhs = nearby(pulls, slots, block, 0, LENGTH)
        pull = pull_even[mine, block + 1].astype(F32)
        scalar_grad = pull + weighted_sum(kern_ref, 0, rhs, scale_two[0])
        scalar_grad = scalar_grad.astype(BF16).astype(F32)
        hidden_grad = (scalar_grad * silu_pair(hidden[block])[1]).astype(BF16)
        inv_grad = turned_dot(hidden_grad, mix[...])
        inv_grad = inv_grad.astype(BF16).astype(F32)
        grads = [inv_grad]
        for d in range(3):
            vector_grad = -weighted_sum(kern_ref, d + 1, rhs, scale_two[1])
            passed = turned_dot(vector_grad.astype(BF16), mixv[...])
            passed = passed.astype(BF16).astype(F32)
            grads.append(passed + 2.0 * vectors[block, d] * inv_grad)
        lane_basis = lax.broadcasted_iota(jnp.int32, (LENGTH, LENGTH), 1) >> 3
        for r in range(4):
            which = min(r, 1)
            spread = jnp.concatenate(
                [table * scale_one[which][b : b + 1, :] for b in range(BASIS)]
                + [jnp.zeros((LENGTH - 8 * BASIS, LENGTH), F32)],
                axis=0,
            )
            table_grad = turned_dot(grads[r], spread, precision=lax.Precision.HIGHEST)
            for b in range(BASIS):
                at = r * depth + b * LENGTH
                scaled = pull * scale_two[which][b : b + 1, :]
                lhs_ref[at : at + LENGTH, :LENGTH] = scaled.astype(BF16)
                lhs_ref[at : at + LENGTH, LENGTH:] = jnp.where(
                    lane_basis == b, table_grad, 0.0
                ).astype(BF16)
        row_ref[...] = jnp.zeros(row_ref.shape, F32)
        rows = 16
        for tile in range(3):
            for near in range(3):
                for r in range(4):
                    sender = jnp.concatenate(
                        [
                            feats[tile][0, block + near, r * LENGTH : (r + 1) * LENGTH, :],
                            hot_ref[tile, block + near],
                        ],
                        axis=1,
                    )
                    deriv_ref[r * depth : (r + 1) * depth, :] = turned_dot(
                        lhs_ref[r * depth : (r + 1) * depth, :], sender
                    )
                cell = (block + near) * 3 + tile

                def chain(step, columns):
                    first = pl.multiple_of(step * rows, rows)
                    apart, eight, centred, gauss, ratio, rest = pair_geometry(
                        send_ref, recv_ref, block, cell, first, rows
                    )
                    if tile == 1 and near == 1:
                        own = first + lax.broadcasted_iota(jnp.int32, (rows, LENGTH), 0)
                        other = lax.broadcasted_iota(jnp.int32, (rows, LENGTH), 1)
                        rest = jnp.where(own == other, 0.0, rest)
                    along = [None, None, None]
                    value = None
                    slope = None
                    for b in range(BASIS - 1, -1, -1):
                        parts = [
                            deriv_ref[pl.ds(r * depth + b * LENGTH + first, rows), :]
                            for r in range(4)
                        ]
                        joint = parts[0]
                        for d in range(3):
                            joint = joint + apart[d] * parts[d + 1]
                            along[d] = (
                                parts[d + 1]
                                if along[d] is None
                                else along[d] * ratio + parts[d + 1]
                            )
                        if value is None:
                            value = joint
                        else:
                            slope = value if slope is None else slope * ratio + value
                            value = value * ratio + joint
                    slope = slope * ratio
                    scale = gauss * rest
                    radial = (
                        scale * (8.0 * rest * (slope - centred * value) - 2.0 * value)
                    ) * (2.0 * INV_CUTOFF)
                    envelope = scale * rest * INV_CUTOFF
                    out = []
                    for d in range(3):
                        pushed = envelope * along[d] + radial * apart[d]
                        row_ref[d, pl.ds(first, rows), :] = (
                            row_ref[d, pl.ds(first, rows), :] + pushed
                        )
                        out.append(columns[d] + pushed)
                    return tuple(out)

                zero = jnp.zeros((rows, LENGTH), F32)
                columns = lax.fori_loop(0, LENGTH // rows, chain, (zero, zero, zero))
                for d in range(3):
                    force_out[tile, block + near, d : d + 1, :] = force_out[
                        tile, block + near, d : d + 1, :
                    ] - jnp.sum(columns[d], axis=0, keepdims=True)
        for d in range(3):
            total = jnp.sum(jnp.transpose(row_ref[d]), axis=0, keepdims=True)
            force_out[1, block + 1, d : d + 1, :] = (
                force_out[1, block + 1, d : d + 1, :] + total
            )
        return carry

    lax.fori_loop(0, 2, body, 0)


AXES = ("slab", "tile")


class Grid:
    def __init__(self, slabs, tiles):
        self.slabs, self.tiles = slabs, tiles
        self.moved = (slabs, tiles) == (16, 32)
        self.cycle = [(x, y) for y in range(4) for x in ((1, 2, 3) if y % 2 == 0 else (3, 2, 1))]
        self.cycle += [(0, y) for y in (3, 2, 1, 0)]

    def device(self, slab, tile):
        slab, tile = slab % self.slabs, tile % self.tiles
        if self.moved:
            x, y = self.cycle[slab]
            z, core = tile // 2, (tile // 2 + tile) % 2
            slab, tile = x * 4 + z % 4, ((z // 4) * 4 + y) * 2 + core
        return slab * self.tiles + tile

    def places(self):
        return [(slab, tile) for slab in range(self.slabs) for tile in range(self.tiles)]

    def flag(self):
        odd = lax.axis_index("tile")
        if self.moved:
            odd = odd + lax.axis_index("slab")
        return (1 - odd % 2).astype(jnp.int32)

    def to_work(self, block):
        if not self.moved:
            return block
        route = [(s * self.tiles + t, self.device(s, t)) for s, t in self.places()]
        return lax.ppermute(block, AXES, route)

    def to_owner(self, block):
        if not self.moved:
            return block
        route = [(self.device(s, t), s * self.tiles + t) for s, t in self.places()]
        return lax.ppermute(block, AXES, route)

    def along_slab(self, block, step):
        route = [(self.device(s, t), self.device(s + step, t)) for s, t in self.places()]
        return lax.ppermute(block, AXES, route)

    def with_partner(self, block, odd):
        groups = [
            [self.device(s, t + odd), self.device(s, t + odd + 1)]
            for s, t in self.places()
            if t % 2 == 0
        ]
        return lax.all_gather(block, AXES, axis_index_groups=groups)

    def swap(self, block, odd):
        route = []
        for s, t in self.places():
            if t % 2 == 0:
                ends = self.device(s, t + odd), self.device(s, t + odd + 1)
                route += [ends, ends[::-1]]
        return lax.ppermute(block, AXES, route)

    def column(self, cells):
        above = self.along_slab(cells[1:], 1)
        below = self.along_slab(cells[:1], -1)
        return jnp.concatenate([above, cells, below], axis=0)

    def gather_near(self, cells):
        column = self.column(cells)
        return self.with_partner(column, 0), self.with_partner(column, 1)

    def swap_near(self, cells):
        column = self.column(cells)[None]
        return self.swap(column, 0), column, self.swap(column, 1)

    def send_home(self, parts, flag):
        even = self.with_partner(parts[0], 0)
        odd = self.with_partner(parts[2], 1)
        column = (
            parts[1]
            + lax.dynamic_index_in_dim(even, flag, 0, False)
            + lax.dynamic_index_in_dim(odd, 1 - flag, 0, False)
        )
        from_next = self.along_slab(column[:1], -1)
        from_last = self.along_slab(column[3:], 1)
        return column[1:3] + jnp.concatenate([from_last, from_next], axis=0)


def kernel_call(body, outs, scratch, flops, operands):
    in_specs = [pl.BlockSpec(memory_space=pltpu.SMEM)]
    in_specs += [pl.BlockSpec(memory_space=pltpu.VMEM)] * (operands - 1)
    return pl.pallas_call(
        body,
        out_shape=[jax.ShapeDtypeStruct(shape, kind) for shape, kind in outs],
        in_specs=in_specs,
        out_specs=[pl.BlockSpec(memory_space=pltpu.VMEM)] * len(outs),
        scratch_shapes=[pltpu.VMEM(shape, kind) for shape, kind in scratch],
        compiler_params=pltpu.CompilerParams(vmem_limit_bytes=VMEM_LIMIT),
        cost_estimate=pl.CostEstimate(flops=flops, bytes_accessed=1 << 20, transcendentals=0),
    )


GEOMETRY = [
    ((12, 3, LENGTH), F32),
    ((2, 3, LENGTH, LENGTH), F32),
    ((4 * BASIS * LENGTH, NEAR * LENGTH), BF16),
]


def first_call():
    outs = [
        ((2, 4 * LENGTH, LENGTH), BF16),
        ((2, LENGTH, LENGTH), F32),
        ((2, 3, LENGTH, LENGTH), F32),
    ]
    scratch = GEOMETRY + [((3, 4, LENGTH, LENGTH), BF16)]
    return kernel_call(first_kernel, outs, scratch, 2400000000, 7)


def second_call():
    outs = [((2, 1, LENGTH), F32), ((2, LENGTH, LENGTH), BF16)]
    return kernel_call(second_kernel, outs, GEOMETRY, 2400000000, 9)


def third_call():
    scratch = GEOMETRY + [
        ((3, 4, LENGTH, LENGTH), BF16),
        ((4 * BASIS * LENGTH, 2 * LENGTH), BF16),
        ((4 * BASIS * LENGTH, LENGTH), F32),
        ((3, LENGTH, LENGTH), F32),
    ]
    return kernel_call(third_kernel, [((3, 4, 4, LENGTH), F32)], scratch, 7200000000, 16)


def on_device(
    grid, positions, species, occupied, embedding, first_radial_weight, radial_two, mix_scalar,
    vector_channel_weight, out_weight, read_weight,
):
    codes = jnp.where(occupied > 0, species, -1).astype(F32)
    packet = jnp.concatenate([positions, codes[:, :, None]], axis=2)[:, 0]
    flag = grid.flag()
    places = (flag[None], *grid.gather_near(grid.to_work(packet)))
    features, hidden, vectors = first_call()(
        *places, embedding, first_radial_weight, mix_scalar, vector_channel_weight
    )
    near_features = grid.swap_near(features)
    energies, pull = second_call()(
        *places, *near_features, radial_two, out_weight, read_weight[None, :]
    )
    near_pulls = grid.gather_near(pull)
    (parts,) = third_call()(
        *places, *near_features, *near_pulls, hidden, vectors, energies, embedding,
        first_radial_weight, radial_two, mix_scalar, vector_channel_weight,
    )
    final = grid.to_owner(grid.send_home(parts, flag))
    return final[:, 3:], final[:, None, :3]


def solution(mesh):
    grid = Grid(mesh.shape["slab"], mesh.shape["tile"])
    in_specs = (
        P("slab", "tile", None, None),
        P("slab", "tile", None),
        P("slab", "tile", None),
        P(),
        P(),
        P(),
        P(),
        P(),
        P(),
        P(),
    )
    out_specs = (P("slab", "tile", None), P("slab", "tile", None, None))
    return jax.shard_map(
        functools.partial(on_device, grid), mesh=mesh, in_specs=in_specs, out_specs=out_specs, check_vma=False
    )
```

```python
import functools

import jax
import jax.numpy as jnp
from jax import lax
from jax.experimental import pallas as pl
from jax.experimental.pallas import tpu as pltpu
from jax.sharding import PartitionSpec as P

F32 = jnp.float32
BF16 = jnp.bfloat16
LENGTH = 128
BASIS = 8
NEAR = 9
FAR = 1000.0
INV_CUTOFF = 0.2
CELL_SLAB = 5.0
CELL_TILE = 10.0


def silu_pair(value):
    gate = 1.0 / (1.0 + jnp.exp(-value))
    return value * gate, gate * (1.0 + value * (1.0 - gate))


OWN_SLOTS = ((0, 0), (1, 0), (2, 0))


def slots_of(flag_ref):
    flag = flag_ref[0]
    turn = (2 * flag - 1).astype(F32) * CELL_TILE
    return ((0, flag), (0, 1 - flag), (1, 1 - flag)), (turn, 0.0, -turn)


def across_lanes(rows, count):
    turned = jnp.transpose(rows)
    return [jnp.broadcast_to(turned[:, k : k + 1], (LENGTH, LENGTH)) for k in range(count)]


def stacked(rows):
    filled = sum(row.shape[0] for row in rows)
    return jnp.concatenate(rows + [jnp.zeros((LENGTH - filled, LENGTH), F32)], axis=0)


def place_atoms(pairs, slots, turns, send_ref, recv_ref):
    rows = []
    for row in range(4):
        for tile in range(3):
            ref, member = pairs[slots[tile][0]], slots[tile][1]
            cell = ref[member, row]
            real = cell[3:4] > -0.5
            shift = ((row - 1) * CELL_SLAB, turns[tile], 0.0)
            for d in range(3):
                coords = cell[d : d + 1] + shift[d]
                rows.append(jnp.where(real, coords, -FAR) * INV_CUTOFF)
                if tile == 1 and row in (1, 2):
                    recv_ref[row - 1, d : d + 1, :] = jnp.where(real, coords, FAR) * INV_CUTOFF
    for k, column in enumerate(across_lanes(stacked(rows), 36)):
        send_ref[k // 3, k % 3] = column


def folded(weights, which):
    order = lax.broadcasted_iota(jnp.int32, (BASIS, LENGTH), 0).astype(F32)
    return weights[which] * jnp.exp(-0.5 * order * (order + 1.0))


def place_weights(weights, column_ref):
    rows = stacked([folded(weights, which) for which in range(2)])
    for k, column in enumerate(across_lanes(rows, 2 * BASIS)):
        column_ref[k] = column


def banked(bank):
    return bank.at[:LENGTH], bank.at[LENGTH : 2 * LENGTH], bank.at[2 * LENGTH :]


def species_rows(embedding):
    return embedding[...].astype(F32)[:8]


def species_hot(code_row):
    order = lax.broadcasted_iota(jnp.int32, (LENGTH, LENGTH), 0)
    species = (order & 7).astype(F32)
    return jnp.where(code_row == species, 1.0, 0.0).astype(BF16)


def plain_dot(lhs, rhs, **kinds):
    return jnp.dot(lhs, rhs, preferred_element_type=F32, **kinds)


def turned_dot(lhs, rhs):
    return lax.dot_general(lhs, rhs, (((0,), (0,)), ((), ())), preferred_element_type=F32)


def pair_geometry(send_ref, recv_ref, block, cell, first, rows, hidden_from):
    apart = [
        send_ref[cell, d, pl.ds(first, rows), :] - recv_ref[block, d : d + 1, :] for d in range(3)
    ]
    square = apart[0] * apart[0] + apart[1] * apart[1] + apart[2] * apart[2]
    square = jnp.minimum(square, 1.0)
    eight = 8.0 * square
    centred = eight - 0.5
    rest = 1.0 - square
    if hidden_from is not None:
        sender = first + lax.broadcasted_iota(jnp.int32, (rows, LENGTH), 0)
        receiver = hidden_from + lax.broadcasted_iota(jnp.int32, (rows, LENGTH), 1)
        rest = jnp.where(sender == receiver, 0.0, rest)
    return apart, centred, jnp.exp(-0.5 * centred * centred), jnp.exp(eight), rest


def fill_kernels(send_ref, recv_ref, kern_ref, block):
    rows = 16

    def body(step, carry):
        first = pl.multiple_of(step * rows, rows)
        for tile in range(3):
            for near in range(3):
                own = 0 if tile == 1 and near == 1 else None
                apart, _, gauss, ratio, rest = pair_geometry(
                    send_ref, recv_ref, block, (block + near) * 3 + tile, first, rows, own
                )
                value = gauss * (rest * rest)
                narrow = [a.astype(BF16) for a in apart]
                at = pl.ds(first + (tile * 3 + near) * LENGTH, rows)
                for b in range(BASIS):
                    radial = value.astype(BF16)
                    kern_ref[at, b * LENGTH : (b + 1) * LENGTH] = radial
                    for d in range(3):
                        column = ((d + 1) * BASIS + b) * LENGTH
                        kern_ref[at, column : column + LENGTH] = radial * narrow[d]
                    if b + 1 < BASIS:
                        value = value * ratio
        return carry

    lax.fori_loop(0, LENGTH // rows, body, 0)


def weighted_sum(kern_ref, part, lhs, column_ref):
    depth = BASIS * LENGTH
    product = plain_dot(lhs, kern_ref[:, part * depth : (part + 1) * depth])
    first = min(part, 1) * BASIS
    total = product[:, :LENGTH] * column_ref[first]
    for b in range(1, BASIS):
        total = total + product[:, b * LENGTH : (b + 1) * LENGTH] * column_ref[first + b]
    return total


def nearby(pairs, slots, block, lo):
    return jnp.concatenate(
        [
            pairs[which][member, block + near, lo : lo + LENGTH, :]
            for which, member in slots
            for near in range(3)
        ],
        axis=1,
    )


def first_kernel(
    flag, even, odd, bank, weights, feat_out, hidden_out, vector_out,
    kern_ref, send_ref, recv_ref, column_ref, start_ref,
):
    mix, mixv, embedding = banked(bank)
    pairs = (even, odd)
    slots, turns = slots_of(flag)
    place_atoms(pairs, slots, turns, send_ref, recv_ref)
    place_weights(weights, column_ref)
    table = jnp.concatenate([species_rows(embedding)] * 16, axis=0).astype(BF16)
    for tile in range(3):
        for row in range(4):
            hot = species_hot(pairs[slots[tile][0]][slots[tile][1], row][3:4])
            start_ref[tile, row] = (turned_dot(table, hot) * 0.0625).astype(BF16)

    def body(block, carry):
        fill_kernels(send_ref, recv_ref, kern_ref.at[block], block)
        lhs = jnp.concatenate(
            [start_ref[tile, block + near] for tile in range(3) for near in range(3)], axis=1
        )
        invariant = weighted_sum(kern_ref.at[block], 0, lhs, column_ref)
        for d in range(3):
            vector = weighted_sum(kern_ref.at[block], d + 1, lhs, column_ref)
            vector_out[block, d] = vector
            invariant = invariant + vector * vector
            mixed = turned_dot(mixv[...], vector.astype(BF16))
            feat_out[block, (d + 1) * LENGTH : (d + 2) * LENGTH, :] = mixed.astype(BF16)
        hidden = turned_dot(mix[...], invariant.astype(BF16))
        hidden_out[block] = hidden
        start = start_ref[1, block + 1].astype(F32)
        feat_out[block, :LENGTH, :] = (start + silu_pair(hidden)[0]).astype(BF16)
        return carry

    lax.fori_loop(0, 2, body, 0)


def second_kernel(
    flag, even, feat_even, feat_mine, feat_odd, kern_ref, weights, out_weight, read, energy_out,
    pull_out, column_ref,
):
    slots, _ = slots_of(flag)
    feats = (feat_even, feat_mine, feat_odd)
    place_weights(weights, column_ref)
    mine = slots[1][1]
    (read_column,) = across_lanes(jnp.broadcast_to(read[...], (LENGTH, LENGTH)), 1)

    def body(block, carry):
        message = feat_mine[0, block + 1, :LENGTH, :].astype(F32)
        for r in range(4):
            lhs = nearby(feats, OWN_SLOTS, block, r * LENGTH)
            message = message + weighted_sum(kern_ref.at[block], r, lhs, column_ref)
        hidden = turned_dot(out_weight[...], message.astype(BF16))
        value, slope = silu_pair(hidden)
        present = even[mine, block + 1][3:4] > -0.5
        energy = jnp.sum(value * read_column, axis=0, keepdims=True)
        energy_out[block] = jnp.where(present, energy, 0.0)
        back = jnp.where(present, slope * read_column, 0.0).astype(BF16)
        pull_out[block] = plain_dot(out_weight[...], back).astype(BF16)
        return carry

    lax.fori_loop(0, 2, body, 0)


def pair_kernel(block, send_ref, recv_ref, kern_ref):
    fill_kernels(send_ref, recv_ref, kern_ref, block)


def third_kernel(
    flag, even, odd, send_ref, recv_ref, feat_even, feat_mine, feat_odd, kern_one, kern_two, pull_even, pull_mine, pull_odd,
    hidden, vectors, energies, bank, weights_one, weights_two, force_out,
    column_ref, hot_ref, feat_ref, seed_ref, deriv_even, deriv_odd,
    push_ref, own_ref,
):
    mix, mixv, embedding = banked(bank)
    pairs = (even, odd)
    feats = (feat_even, feat_mine, feat_odd)
    pulls = (pull_even, pull_mine, pull_odd)
    slots, _ = slots_of(flag)
    depth = BASIS * LENGTH
    place_weights(weights_two, column_ref)
    for tile in range(3):
        for row in range(4):
            hot_ref[row * 3 + tile] = species_hot(pairs[slots[tile][0]][slots[tile][1], row][3:4])
    push_ref[...] = jnp.zeros(push_ref.shape, F32)
    own_ref[...] = jnp.zeros(own_ref.shape, F32)
    table = species_rows(embedding)
    spreads = []
    for which in range(2):
        scale = folded(weights_one, which)
        spreads.append(stacked([table * scale[b : b + 1, :] for b in range(BASIS)]))

    def pull_back(block, kern_ref):
        lhs = nearby(pulls, OWN_SLOTS, block, 0)
        pull = pull_mine[0, block + 1].astype(F32)
        scalar_grad = pull + weighted_sum(kern_ref, 0, lhs, column_ref)
        scalar_grad = scalar_grad.astype(BF16).astype(F32)
        hidden_grad = (scalar_grad * silu_pair(hidden[block])[1]).astype(BF16)
        inv_grad = plain_dot(mix[...], hidden_grad)
        inv_grad = inv_grad.astype(BF16).astype(F32)
        grads = [inv_grad]
        for d in range(3):
            vector_grad = -weighted_sum(kern_ref, d + 1, lhs, column_ref)
            passed = plain_dot(mixv[...], vector_grad.astype(BF16))
            passed = passed.astype(BF16).astype(F32)
            grads.append(passed + 2.0 * vectors[block, d] * inv_grad)
        basis = lax.broadcasted_iota(jnp.int32, (LENGTH, LENGTH), 0) >> 3
        for r in range(4):
            which = min(r, 1)
            table_grad = plain_dot(spreads[which], grads[r], precision=lax.Precision.HIGHEST)
            for b in range(BASIS):
                at = r * depth + b * LENGTH
                scaled = pull * column_ref[which * BASIS + b]
                seed_ref[block, :LENGTH, at : at + LENGTH] = scaled.astype(BF16)
                seed_ref[block, LENGTH:, at : at + LENGTH] = jnp.where(
                    basis == b, table_grad, 0.0
                ).astype(BF16)

    pull_back(0, kern_one)
    pull_back(1, kern_two)
    for tile in range(3):
        for row in range(4):
            feat_ref[row * 3 + tile] = feats[tile][0, row]

    def find(pair):
        block = pair // NEAR
        place = pair - block * NEAR
        return block, place, (block + place // 3) * 3 + place % 3

    def differentiate(pair, deriv_ref):
        block, _, cell = find(pair)
        for r in range(4):
            sender = jnp.concatenate(
                [feat_ref[cell, r * LENGTH : (r + 1) * LENGTH, :], hot_ref[cell]], axis=0
            )
            deriv_ref[:, r * depth : (r + 1) * depth] = turned_dot(
                sender, seed_ref[block, :, r * depth : (r + 1) * depth]
            )

    def chain(pair, deriv_ref):
        sums = [jnp.zeros((16, LENGTH), F32)] * 3
        block, place, cell = find(pair)
        hidden_from = jnp.where(place == 4, 0, 4 * LENGTH)
        rows = 16
        for step in range(LENGTH // rows):
            first = step * rows
            apart, centred, gauss, ratio, rest = pair_geometry(
                send_ref, recv_ref, block, cell, first, rows, hidden_from
            )
            along = [None, None, None]
            value = None
            slope = None
            for b in range(BASIS - 1, -1, -1):
                parts = []
                for r in range(4):
                    at = r * depth + b * LENGTH
                    parts.append(deriv_ref[first : first + rows, at : at + LENGTH])
                joint = parts[0]
                for d in range(3):
                    part = parts[d + 1]
                    joint = joint + apart[d] * part
                    along[d] = part if along[d] is None else along[d] * ratio + part
                if value is None:
                    value = joint
                else:
                    slope = value if slope is None else slope * ratio + value
                    value = value * ratio + joint
            slope = slope * ratio
            scale = gauss * rest
            radial = scale * (8.0 * rest * (slope - centred * value) - 2.0 * value)
            radial = radial * (2.0 * INV_CUTOFF)
            envelope = scale * rest * INV_CUTOFF
            for d in range(3):
                pushed = envelope * along[d] + radial * apart[d]
                push_ref[cell, d, first : first + rows, :] += pushed
                sums[d] = sums[d] + pushed
        for d in range(3):
            own_ref[block, d] += sums[d]

    differentiate(0, deriv_even)

    def pair_steps(step, carry):
        pair = step * 2
        differentiate(pair + 1, deriv_odd)
        chain(pair, deriv_even)
        differentiate(jnp.minimum(pair + 2, 2 * NEAR - 1), deriv_even)
        chain(pair + 1, deriv_odd)
        return carry

    lax.fori_loop(0, NEAR, pair_steps, 0)
    force_out[...] = jnp.zeros(force_out.shape, F32)
    ones = jnp.ones((16, 2 * LENGTH), BF16)
    for row in range(4):
        for tile in range(3):
            for d in range(3):
                total = push_ref[row * 3 + tile, d]
                high = total.astype(BF16)
                low = (total - high.astype(F32)).astype(BF16)
                parts = jnp.concatenate([high, low], axis=1)
                pushed = lax.dot_general(
                    ones, parts, (((1,), (1,)), ((), ())), preferred_element_type=F32
                )[:1]
                if tile == 1 and row in (1, 2):
                    pushed = pushed - jnp.sum(own_ref[row - 1, d], axis=0, keepdims=True)
                force_out[tile, row, d : d + 1, :] = -pushed
    for block in range(2):
        force_out[1, block + 1, 3:4, :] = energies[block]


AXES = ("slab", "tile")


class Grid:
    def __init__(self, slabs, tiles):
        self.slabs, self.tiles = slabs, tiles
        self.moved = (slabs, tiles) == (16, 32)
        self.cycle = [(x, y) for y in range(4) for x in ((1, 2, 3) if y % 2 == 0 else (3, 2, 1))]
        self.cycle += [(0, y) for y in (3, 2, 1, 0)]

    def device(self, slab, tile):
        slab, tile = slab % self.slabs, tile % self.tiles
        if self.moved:
            x, y = self.cycle[slab]
            z, core = tile // 2, (tile // 2 + tile) % 2
            slab, tile = x * 4 + z % 4, ((z // 4) * 4 + y) * 2 + core
        return slab * self.tiles + tile

    def places(self):
        return [(slab, tile) for slab in range(self.slabs) for tile in range(self.tiles)]

    def flag(self):
        odd = lax.axis_index("tile")
        if self.moved:
            odd = odd + lax.axis_index("slab")
        return (1 - odd % 2).astype(jnp.int32)

    def to_work(self, block):
        if not self.moved:
            return block
        route = [(s * self.tiles + t, self.device(s, t)) for s, t in self.places()]
        return lax.ppermute(block, AXES, route)

    def to_owner(self, block):
        if not self.moved:
            return block
        route = [(self.device(s, t), s * self.tiles + t) for s, t in self.places()]
        return lax.ppermute(block, AXES, route)

    def along_slab(self, block, step):
        route = [(self.device(s, t), self.device(s + step, t)) for s, t in self.places()]
        return lax.ppermute(block, AXES, route)

    def with_partner(self, block, odd):
        groups = [
            [self.device(s, t + odd), self.device(s, t + odd + 1)]
            for s, t in self.places()
            if t % 2 == 0
        ]
        return lax.all_gather(block, AXES, axis_index_groups=groups)

    def swap(self, block, odd):
        route = []
        for s, t in self.places():
            if t % 2 == 0:
                ends = self.device(s, t + odd), self.device(s, t + odd + 1)
                route += [ends, ends[::-1]]
        return lax.ppermute(block, AXES, route)

    def column(self, cells):
        above = self.along_slab(cells[1:], 1)
        below = self.along_slab(cells[:1], -1)
        return jnp.concatenate([above, cells, below], axis=0)

    def gather_near(self, cells):
        column = self.column(cells)
        return self.with_partner(column, 0), self.with_partner(column, 1)

    def swap_near(self, cells):
        column = self.column(cells)[None]
        return self.swap(column, 0), column, self.swap(column, 1)

    def send_home(self, parts, flag):
        even = self.with_partner(parts[0], 0)
        odd = self.with_partner(parts[2], 1)
        column = (
            parts[1]
            + lax.dynamic_index_in_dim(even, flag, 0, False)
            + lax.dynamic_index_in_dim(odd, 1 - flag, 0, False)
        )
        from_next = self.along_slab(column[:1], -1)
        from_last = self.along_slab(column[3:], 1)
        return column[1:3] + jnp.concatenate([from_last, from_next], axis=0)


def kernel_call(body, outs, scratch, flops, operands, room, flagged=True):
    in_specs = [pl.BlockSpec(memory_space=pltpu.VMEM)] * operands
    if flagged:
        in_specs[0] = pl.BlockSpec(memory_space=pltpu.SMEM)
    return pl.pallas_call(
        body,
        out_shape=[jax.ShapeDtypeStruct(shape, kind) for shape, kind in outs],
        in_specs=in_specs,
        out_specs=[pl.BlockSpec(memory_space=pltpu.VMEM)] * len(outs),
        scratch_shapes=[pltpu.VMEM(shape, kind) for shape, kind in scratch],
        compiler_params=pltpu.CompilerParams(vmem_limit_bytes=room * 1024 * 1024),
        cost_estimate=pl.CostEstimate(flops=flops, bytes_accessed=1 << 20, transcendentals=0),
    )


GEOMETRY = [
    ((12, 3, LENGTH, LENGTH), F32),
    ((2, 3, LENGTH), F32),
    ((2 * BASIS, LENGTH, LENGTH), F32),
]


def first_call():
    outs = [
        ((2, 4 * LENGTH, LENGTH), BF16),
        ((2, LENGTH, LENGTH), F32),
        ((2, 3, LENGTH, LENGTH), F32),
        ((2, NEAR * LENGTH, 4 * BASIS * LENGTH), BF16),
        ((12, 3, LENGTH, LENGTH), F32),
        ((2, 3, LENGTH), F32),
    ]
    scratch = GEOMETRY[2:] + [((3, 4, LENGTH, LENGTH), BF16)]
    return kernel_call(first_kernel, outs, scratch, 2400000000, 5, 18)


def second_call():
    outs = [((2, 1, LENGTH), F32), ((2, LENGTH, LENGTH), BF16)]
    return kernel_call(second_kernel, outs, GEOMETRY[2:], 2400000000, 9, 18)


def pair_call(block):
    outs = [((NEAR * LENGTH, 4 * BASIS * LENGTH), BF16)]
    body = functools.partial(pair_kernel, block)
    return kernel_call(body, outs, [], 900000000, 2, 18, False)


def third_call():
    scratch = GEOMETRY[2:] + [
        ((12, LENGTH, LENGTH), BF16),
        ((12, 4 * LENGTH, LENGTH), BF16),
        ((2, 2 * LENGTH, 4 * BASIS * LENGTH), BF16),
        ((LENGTH, 4 * BASIS * LENGTH), F32),
        ((LENGTH, 4 * BASIS * LENGTH), F32),
        ((12, 3, LENGTH, LENGTH), F32),
        ((2, 3, 16, LENGTH), F32),
    ]
    return kernel_call(third_kernel, [((3, 4, 4, LENGTH), F32)], scratch, 7200000000, 19, 18)


def on_device(
    grid, positions, species, occupied, embedding, first_radial_weight, radial_two, mix_scalar,
    vector_channel_weight, out_weight, read_weight,
):
    codes = jnp.where(occupied > 0, species, -1).astype(F32)
    packet = jnp.concatenate([positions, codes[:, :, None]], axis=2)[:, 0]
    flag = grid.flag()
    spare = jnp.zeros((16 - embedding.shape[0], LENGTH), BF16)
    bank = jnp.concatenate([mix_scalar, vector_channel_weight, embedding, spare], axis=0)
    weights_one = first_radial_weight * 0.25
    weights_two = radial_two * 0.25
    places = (flag[None], *grid.gather_near(grid.to_work(packet)))
    features, hidden, vectors, kernels, senders, receivers = first_call()(
        *places, bank, weights_one
    )
    near_features = grid.swap_near(features)
    energies, pull = second_call()(
        *places[:2], *near_features, kernels, weights_two, out_weight, read_weight[None, :]
    )
    pull, senders, receivers = lax.optimization_barrier((pull, senders, receivers))
    near_pulls = grid.swap_near(pull)
    again = [pair_call(block)(senders, receivers)[0] for block in range(2)]
    (parts,) = third_call()(
        *places, senders, receivers, *near_features, *again, *near_pulls, hidden, vectors, energies, bank,
        weights_one, weights_two,
    )
    final = grid.to_owner(grid.send_home(parts, flag))
    return final[:, 3:], final[:, None, :3]


def solution(mesh):
    grid = Grid(mesh.shape["slab"], mesh.shape["tile"])
    in_specs = (
        P("slab", "tile", None, None),
        P("slab", "tile", None),
        P("slab", "tile", None),
        P(),
        P(),
        P(),
        P(),
        P(),
        P(),
        P(),
    )
    out_specs = (P("slab", "tile", None), P("slab", "tile", None, None))
    return jax.shard_map(
        functools.partial(on_device, grid), mesh=mesh, in_specs=in_specs, out_specs=out_specs, check_vma=False
    )
```

```python
import functools

import jax
import jax.numpy as jnp
from jax import lax
from jax.experimental import pallas as pl
from jax.experimental.pallas import tpu as pltpu
from jax.sharding import PartitionSpec as P

F32 = jnp.float32
BF16 = jnp.bfloat16
LENGTH = 128
BASIS = 8
NEAR = 9
FAR = 1000.0
INV_CUTOFF = 0.2
CELL_SLAB = 5.0
CELL_TILE = 10.0


def silu_pair(value):
    gate = 1.0 / (1.0 + jnp.exp(-value))
    return value * gate, gate * (1.0 + value * (1.0 - gate))


OWN_SLOTS = ((0, 0), (1, 0), (2, 0))


def slots_of(flag_ref):
    flag = flag_ref[0]
    turn = (2 * flag - 1).astype(F32) * CELL_TILE
    return ((0, flag), (0, 1 - flag), (1, 1 - flag)), (turn, 0.0, -turn)


def across_lanes(rows, count):
    turned = jnp.transpose(rows)
    return [jnp.broadcast_to(turned[:, k : k + 1], (LENGTH, LENGTH)) for k in range(count)]


def stacked(rows):
    filled = sum(row.shape[0] for row in rows)
    return jnp.concatenate(rows + [jnp.zeros((LENGTH - filled, LENGTH), F32)], axis=0)


def place_atoms(pairs, slots, turns, send_ref, recv_ref):
    rows = []
    for row in range(4):
        for tile in range(3):
            ref, member = pairs[slots[tile][0]], slots[tile][1]
            cell = ref[member, row]
            real = cell[3:4] > -0.5
            shift = ((row - 1) * CELL_SLAB, turns[tile], 0.0)
            for d in range(3):
                coords = cell[d : d + 1] + shift[d]
                rows.append(jnp.where(real, coords, -FAR) * INV_CUTOFF)
                if tile == 1 and row in (1, 2):
                    recv_ref[row - 1, d : d + 1, :] = jnp.where(real, coords, FAR) * INV_CUTOFF
    for k, column in enumerate(across_lanes(stacked(rows), 36)):
        send_ref[k // 3, k % 3] = column


def folded(weights, which):
    order = lax.broadcasted_iota(jnp.int32, (BASIS, LENGTH), 0).astype(F32)
    return weights[which] * jnp.exp(-0.5 * order * (order + 1.0))


def place_weights(weights, column_ref):
    rows = stacked([folded(weights, which) for which in range(2)])
    for k, column in enumerate(across_lanes(rows, 2 * BASIS)):
        column_ref[k] = column


def banked(bank):
    return bank.at[:LENGTH], bank.at[LENGTH : 2 * LENGTH], bank.at[2 * LENGTH :]


def species_rows(embedding):
    return embedding[...].astype(F32)[:8]


def species_hot(code_row):
    order = lax.broadcasted_iota(jnp.int32, (LENGTH, LENGTH), 0)
    species = (order & 7).astype(F32)
    return jnp.where(code_row == species, 1.0, 0.0).astype(BF16)


def plain_dot(lhs, rhs, **kinds):
    return jnp.dot(lhs, rhs, preferred_element_type=F32, **kinds)


def turned_dot(lhs, rhs):
    return lax.dot_general(lhs, rhs, (((0,), (0,)), ((), ())), preferred_element_type=F32)


def pair_geometry(send_ref, recv_ref, block, cell, first, rows, hidden_from):
    apart = [
        send_ref[cell, d, pl.ds(first, rows), :] - recv_ref[block, d : d + 1, :] for d in range(3)
    ]
    square = apart[0] * apart[0] + apart[1] * apart[1] + apart[2] * apart[2]
    square = jnp.minimum(square, 1.0)
    eight = 8.0 * square
    centred = eight - 0.5
    rest = 1.0 - square
    if hidden_from is not None:
        sender = first + lax.broadcasted_iota(jnp.int32, (rows, LENGTH), 0)
        receiver = hidden_from + lax.broadcasted_iota(jnp.int32, (rows, LENGTH), 1)
        rest = jnp.where(sender == receiver, 0.0, rest)
    return apart, centred, jnp.exp(-0.5 * centred * centred), jnp.exp(eight), rest


def fill_kernels(send_ref, recv_ref, kern_ref, block):
    rows = 16

    def body(step, carry):
        first = pl.multiple_of(step * rows, rows)
        for tile in range(3):
            for near in range(3):
                own = 0 if tile == 1 and near == 1 else None
                apart, _, gauss, ratio, rest = pair_geometry(
                    send_ref, recv_ref, block, (block + near) * 3 + tile, first, rows, own
                )
                value = gauss * (rest * rest)
                narrow = [a.astype(BF16) for a in apart]
                at = pl.ds(first + (tile * 3 + near) * LENGTH, rows)
                for b in range(BASIS):
                    radial = value.astype(BF16)
                    kern_ref[at, b * LENGTH : (b + 1) * LENGTH] = radial
                    for d in range(3):
                        column = ((d + 1) * BASIS + b) * LENGTH
                        kern_ref[at, column : column + LENGTH] = radial * narrow[d]
                    if b + 1 < BASIS:
                        value = value * ratio
        return carry

    lax.fori_loop(0, LENGTH // rows, body, 0)


def weighted_sum(kern_ref, part, lhs, column_ref):
    depth = BASIS * LENGTH
    product = plain_dot(lhs, kern_ref[:, part * depth : (part + 1) * depth])
    first = min(part, 1) * BASIS
    total = product[:, :LENGTH] * column_ref[first]
    for b in range(1, BASIS):
        total = total + product[:, b * LENGTH : (b + 1) * LENGTH] * column_ref[first + b]
    return total


def nearby(pairs, slots, block, lo):
    return jnp.concatenate(
        [
            pairs[which][member, block + near, lo : lo + LENGTH, :]
            for which, member in slots
            for near in range(3)
        ],
        axis=1,
    )


def first_kernel(
    flag, even, odd, bank, weights, feat_out, hidden_out, vector_out,
    kern_ref, send_ref, recv_ref, column_ref, start_ref,
):
    mix, mixv, embedding = banked(bank)
    pairs = (even, odd)
    slots, turns = slots_of(flag)
    place_atoms(pairs, slots, turns, send_ref, recv_ref)
    place_weights(weights, column_ref)
    table = jnp.concatenate([species_rows(embedding)] * 16, axis=0).astype(BF16)
    for tile in range(3):
        for row in range(4):
            hot = species_hot(pairs[slots[tile][0]][slots[tile][1], row][3:4])
            start_ref[tile, row] = (turned_dot(table, hot) * 0.0625).astype(BF16)

    def body(block, carry):
        fill_kernels(send_ref, recv_ref, kern_ref.at[block], block)
        lhs = jnp.concatenate(
            [start_ref[tile, block + near] for tile in range(3) for near in range(3)], axis=1
        )
        invariant = weighted_sum(kern_ref.at[block], 0, lhs, column_ref)
        for d in range(3):
            vector = weighted_sum(kern_ref.at[block], d + 1, lhs, column_ref)
            vector_out[block, d] = vector
            invariant = invariant + vector * vector
            mixed = turned_dot(mixv[...], vector.astype(BF16))
            feat_out[block, (d + 1) * LENGTH : (d + 2) * LENGTH, :] = mixed.astype(BF16)
        hidden = turned_dot(mix[...], invariant.astype(BF16))
        hidden_out[block] = hidden
        start = start_ref[1, block + 1].astype(F32)
        feat_out[block, :LENGTH, :] = (start + silu_pair(hidden)[0]).astype(BF16)
        return carry

    lax.fori_loop(0, 2, body, 0)


def second_kernel(
    flag, even, feat_even, feat_mine, feat_odd, kern_ref, weights, out_weight, read, energy_out,
    pull_out, column_ref,
):
    slots, _ = slots_of(flag)
    feats = (feat_even, feat_mine, feat_odd)
    place_weights(weights, column_ref)
    mine = slots[1][1]
    (read_column,) = across_lanes(jnp.broadcast_to(read[...], (LENGTH, LENGTH)), 1)

    def body(block, carry):
        message = feat_mine[0, block + 1, :LENGTH, :].astype(F32)
        for r in range(4):
            lhs = nearby(feats, OWN_SLOTS, block, r * LENGTH)
            message = message + weighted_sum(kern_ref.at[block], r, lhs, column_ref)
        hidden = turned_dot(out_weight[...], message.astype(BF16))
        value, slope = silu_pair(hidden)
        present = even[mine, block + 1][3:4] > -0.5
        energy = jnp.sum(value * read_column, axis=0, keepdims=True)
        energy_out[block] = jnp.where(present, energy, 0.0)
        back = jnp.where(present, slope * read_column, 0.0).astype(BF16)
        pull_out[block] = plain_dot(out_weight[...], back).astype(BF16)
        return carry

    lax.fori_loop(0, 2, body, 0)


def pair_kernel(block, send_ref, recv_ref, kern_ref):
    fill_kernels(send_ref, recv_ref, kern_ref, block)


def third_kernel(
    flag, even, odd, send_ref, recv_ref, feat_even, feat_mine, feat_odd, kern_one, kern_two, pull_even, pull_mine, pull_odd,
    hidden, vectors, energies, bank, weights_one, weights_two, force_out,
    column_ref, hot_ref, feat_ref, seed_ref, deriv_even, deriv_odd,
    push_ref, own_ref,
):
    mix, mixv, embedding = banked(bank)
    pairs = (even, odd)
    feats = (feat_even, feat_mine, feat_odd)
    pulls = (pull_even, pull_mine, pull_odd)
    slots, _ = slots_of(flag)
    depth = BASIS * LENGTH
    place_weights(weights_two, column_ref)
    for tile in range(3):
        for row in range(4):
            hot_ref[row * 3 + tile] = species_hot(pairs[slots[tile][0]][slots[tile][1], row][3:4])
    push_ref[...] = jnp.zeros(push_ref.shape, F32)
    own_ref[...] = jnp.zeros(own_ref.shape, F32)
    table = species_rows(embedding)
    spreads = []
    for which in range(2):
        scale = folded(weights_one, which)
        spreads.append(stacked([table * scale[b : b + 1, :] for b in range(BASIS)]))

    def pull_back(block, kern_ref):
        lhs = nearby(pulls, OWN_SLOTS, block, 0)
        pull = pull_mine[0, block + 1].astype(F32)
        scalar_grad = pull + weighted_sum(kern_ref, 0, lhs, column_ref)
        scalar_grad = scalar_grad.astype(BF16).astype(F32)
        hidden_grad = (scalar_grad * silu_pair(hidden[block])[1]).astype(BF16)
        inv_grad = plain_dot(mix[...], hidden_grad)
        inv_grad = inv_grad.astype(BF16).astype(F32)
        grads = [inv_grad]
        for d in range(3):
            vector_grad = -weighted_sum(kern_ref, d + 1, lhs, column_ref)
            passed = plain_dot(mixv[...], vector_grad.astype(BF16))
            passed = passed.astype(BF16).astype(F32)
            grads.append(passed + 2.0 * vectors[block, d] * inv_grad)
        basis = lax.broadcasted_iota(jnp.int32, (LENGTH, LENGTH), 0) >> 3
        for r in range(4):
            which = min(r, 1)
            table_grad = plain_dot(spreads[which], grads[r], precision=lax.Precision.HIGHEST)
            for b in range(BASIS):
                at = r * depth + b * LENGTH
                scaled = pull * column_ref[which * BASIS + b]
                seed_ref[block, :LENGTH, at : at + LENGTH] = scaled.astype(BF16)
                seed_ref[block, LENGTH:, at : at + LENGTH] = jnp.where(
                    basis == b, table_grad, 0.0
                ).astype(BF16)

    pull_back(0, kern_one)
    pull_back(1, kern_two)
    for tile in range(3):
        for row in range(4):
            feat_ref[row * 3 + tile] = feats[tile][0, row]

    def find(pair):
        block = pair // NEAR
        place = pair - block * NEAR
        return block, place, (block + place // 3) * 3 + place % 3

    def differentiate(pair, deriv_ref):
        block, _, cell = find(pair)
        for r in range(4):
            sender = jnp.concatenate(
                [feat_ref[cell, r * LENGTH : (r + 1) * LENGTH, :], hot_ref[cell]], axis=0
            )
            deriv_ref[:, r * depth : (r + 1) * depth] = turned_dot(
                sender, seed_ref[block, :, r * depth : (r + 1) * depth]
            )

    def chain(pair, deriv_ref):
        sums = [jnp.zeros((16, LENGTH), F32)] * 3
        block, place, cell = find(pair)
        hidden_from = jnp.where(place == 4, 0, 4 * LENGTH)
        rows = 16
        for step in range(LENGTH // rows):
            first = step * rows
            apart, centred, gauss, ratio, rest = pair_geometry(
                send_ref, recv_ref, block, cell, first, rows, hidden_from
            )
            along = [None, None, None]
            value = None
            slope = None
            for b in range(BASIS - 1, -1, -1):
                parts = []
                for r in range(4):
                    at = r * depth + b * LENGTH
                    parts.append(deriv_ref[first : first + rows, at : at + LENGTH])
                joint = parts[0]
                for d in range(3):
                    part = parts[d + 1]
                    joint = joint + apart[d] * part
                    along[d] = part if along[d] is None else along[d] * ratio + part
                if value is None:
                    value = joint
                else:
                    slope = value if slope is None else slope * ratio + value
                    value = value * ratio + joint
            slope = slope * ratio
            scale = gauss * rest
            radial = scale * (8.0 * rest * (slope - centred * value) - 2.0 * value)
            radial = radial * (2.0 * INV_CUTOFF)
            envelope = scale * rest * INV_CUTOFF
            for d in range(3):
                pushed = envelope * along[d] + radial * apart[d]
                push_ref[cell, d, first : first + rows, :] += pushed
                sums[d] = sums[d] + pushed
        for d in range(3):
            own_ref[block, d] += sums[d]

    differentiate(0, deriv_even)

    def pair_steps(step, carry):
        pair = step * 2
        differentiate(pair + 1, deriv_odd)
        chain(pair, deriv_even)
        differentiate(jnp.minimum(pair + 2, 2 * NEAR - 1), deriv_even)
        chain(pair + 1, deriv_odd)
        return carry

    lax.fori_loop(0, NEAR, pair_steps, 0)
    force_out[...] = jnp.zeros(force_out.shape, F32)
    ones = jnp.ones((16, 2 * LENGTH), BF16)
    for row in range(4):
        for tile in range(3):
            for d in range(3):
                total = push_ref[row * 3 + tile, d]
                high = total.astype(BF16)
                low = (total - high.astype(F32)).astype(BF16)
                parts = jnp.concatenate([high, low], axis=1)
                pushed = lax.dot_general(
                    ones, parts, (((1,), (1,)), ((), ())), preferred_element_type=F32
                )[:1]
                if tile == 1 and row in (1, 2):
                    pushed = pushed - jnp.sum(own_ref[row - 1, d], axis=0, keepdims=True)
                force_out[tile, row, d : d + 1, :] = -pushed
    for block in range(2):
        force_out[1, block + 1, 3:4, :] = energies[block]


AXES = ("slab", "tile")


class Grid:
    def __init__(self, slabs, tiles):
        self.slabs, self.tiles = slabs, tiles
        self.moved = (slabs, tiles) == (16, 32)
        self.cycle = [(0, 0), (0, 1), (0, 2), (0, 3), (1, 3), (1, 2), (1, 1), (2, 1)]
        self.cycle += [(2, 2), (2, 3), (3, 3), (3, 2), (3, 1), (3, 0), (2, 0), (1, 0)]

    def device(self, slab, tile):
        slab, tile = slab % self.slabs, tile % self.tiles
        if self.moved:
            x, y = self.cycle[slab]
            z, core = tile // 2, (tile // 2 + tile) % 2
            slab, tile = x * 4 + z % 4, ((z // 4) * 4 + y) * 2 + core
        return slab * self.tiles + tile

    def places(self):
        return [(slab, tile) for slab in range(self.slabs) for tile in range(self.tiles)]

    def flag(self):
        odd = lax.axis_index("tile")
        if self.moved:
            odd = odd + lax.axis_index("slab")
        return (1 - odd % 2).astype(jnp.int32)

    def to_work(self, block):
        if not self.moved:
            return block
        route = [(s * self.tiles + t, self.device(s, t)) for s, t in self.places()]
        return lax.ppermute(block, AXES, route)

    def to_owner(self, block):
        if not self.moved:
            return block
        route = [(self.device(s, t), s * self.tiles + t) for s, t in self.places()]
        return lax.ppermute(block, AXES, route)

    def along_slab(self, block, step):
        route = [(self.device(s, t), self.device(s + step, t)) for s, t in self.places()]
        return lax.ppermute(block, AXES, route)

    def with_partner(self, block, odd):
        groups = [
            [self.device(s, t + odd), self.device(s, t + odd + 1)]
            for s, t in self.places()
            if t % 2 == 0
        ]
        return lax.all_gather(block, AXES, axis_index_groups=groups)

    def swap(self, block, odd):
        route = []
        for s, t in self.places():
            if t % 2 == 0:
                ends = self.device(s, t + odd), self.device(s, t + odd + 1)
                route += [ends, ends[::-1]]
        return lax.ppermute(block, AXES, route)

    def column(self, cells):
        above = self.along_slab(cells[1:], 1)
        below = self.along_slab(cells[:1], -1)
        return jnp.concatenate([above, cells, below], axis=0)

    def gather_near(self, cells):
        column = self.column(cells)
        return self.with_partner(column, 0), self.with_partner(column, 1)

    def swap_near(self, cells):
        column = self.column(cells)[None]
        return self.swap(column, 0), column, self.swap(column, 1)

    def send_home(self, parts, flag):
        even = self.with_partner(parts[0], 0)
        odd = self.with_partner(parts[2], 1)
        column = (
            parts[1]
            + lax.dynamic_index_in_dim(even, flag, 0, False)
            + lax.dynamic_index_in_dim(odd, 1 - flag, 0, False)
        )
        from_next = self.along_slab(column[:1], -1)
        from_last = self.along_slab(column[3:], 1)
        return column[1:3] + jnp.concatenate([from_last, from_next], axis=0)


def kernel_call(body, outs, scratch, flops, operands, room, flagged=True):
    in_specs = [pl.BlockSpec(memory_space=pltpu.VMEM)] * operands
    if flagged:
        in_specs[0] = pl.BlockSpec(memory_space=pltpu.SMEM)
    return pl.pallas_call(
        body,
        out_shape=[jax.ShapeDtypeStruct(shape, kind) for shape, kind in outs],
        in_specs=in_specs,
        out_specs=[pl.BlockSpec(memory_space=pltpu.VMEM)] * len(outs),
        scratch_shapes=[pltpu.VMEM(shape, kind) for shape, kind in scratch],
        compiler_params=pltpu.CompilerParams(vmem_limit_bytes=room * 1024 * 1024),
        cost_estimate=pl.CostEstimate(flops=flops, bytes_accessed=1 << 20, transcendentals=0),
    )


GEOMETRY = [
    ((12, 3, LENGTH, LENGTH), F32),
    ((2, 3, LENGTH), F32),
    ((2 * BASIS, LENGTH, LENGTH), F32),
]


def first_call():
    outs = [
        ((2, 4 * LENGTH, LENGTH), BF16),
        ((2, LENGTH, LENGTH), F32),
        ((2, 3, LENGTH, LENGTH), F32),
        ((2, NEAR * LENGTH, 4 * BASIS * LENGTH), BF16),
        ((12, 3, LENGTH, LENGTH), F32),
        ((2, 3, LENGTH), F32),
    ]
    scratch = GEOMETRY[2:] + [((3, 4, LENGTH, LENGTH), BF16)]
    return kernel_call(first_kernel, outs, scratch, 2400000000, 5, 18)


def second_call():
    outs = [((2, 1, LENGTH), F32), ((2, LENGTH, LENGTH), BF16)]
    return kernel_call(second_kernel, outs, GEOMETRY[2:], 2400000000, 9, 18)


def pair_call(block):
    outs = [((NEAR * LENGTH, 4 * BASIS * LENGTH), BF16)]
    body = functools.partial(pair_kernel, block)
    return kernel_call(body, outs, [], 900000000, 2, 18, False)


def third_call():
    scratch = GEOMETRY[2:] + [
        ((12, LENGTH, LENGTH), BF16),
        ((12, 4 * LENGTH, LENGTH), BF16),
        ((2, 2 * LENGTH, 4 * BASIS * LENGTH), BF16),
        ((LENGTH, 4 * BASIS * LENGTH), F32),
        ((LENGTH, 4 * BASIS * LENGTH), F32),
        ((12, 3, LENGTH, LENGTH), F32),
        ((2, 3, 16, LENGTH), F32),
    ]
    return kernel_call(third_kernel, [((3, 4, 4, LENGTH), F32)], scratch, 7200000000, 19, 18)


def on_device(
    grid, positions, species, occupied, embedding, first_radial_weight, radial_two, mix_scalar,
    vector_channel_weight, out_weight, read_weight,
):
    codes = jnp.where(occupied > 0, species, -1).astype(F32)
    packet = jnp.concatenate([positions, codes[:, :, None]], axis=2)[:, 0]
    flag = grid.flag()
    spare = jnp.zeros((16 - embedding.shape[0], LENGTH), BF16)
    bank = jnp.concatenate([mix_scalar, vector_channel_weight, embedding, spare], axis=0)
    weights_one = first_radial_weight * 0.25
    weights_two = radial_two * 0.25
    places = (flag[None], *grid.gather_near(grid.to_work(packet)))
    features, hidden, vectors, kernels, senders, receivers = first_call()(
        *places, bank, weights_one
    )
    near_features = grid.swap_near(features)
    energies, pull = second_call()(
        *places[:2], *near_features, kernels, weights_two, out_weight, read_weight[None, :]
    )
    pull, senders, receivers = lax.optimization_barrier((pull, senders, receivers))
    near_pulls = grid.swap_near(pull)
    again = [pair_call(block)(senders, receivers)[0] for block in range(2)]
    (parts,) = third_call()(
        *places, senders, receivers, *near_features, *again, *near_pulls, hidden, vectors, energies, bank,
        weights_one, weights_two,
    )
    final = grid.to_owner(grid.send_home(parts, flag))
    return final[:, 3:], final[:, None, :3]


def solution(mesh):
    grid = Grid(mesh.shape["slab"], mesh.shape["tile"])
    in_specs = (
        P("slab", "tile", None, None),
        P("slab", "tile", None),
        P("slab", "tile", None),
        P(),
        P(),
        P(),
        P(),
        P(),
        P(),
        P(),
    )
    out_specs = (P("slab", "tile", None), P("slab", "tile", None, None))
    return jax.shard_map(
        functools.partial(on_device, grid), mesh=mesh, in_specs=in_specs, out_specs=out_specs, check_vma=False
    )
```

```python
import functools

import jax
import jax.numpy as jnp
from jax import lax
from jax.experimental import pallas as pl
from jax.experimental.pallas import tpu as pltpu
from jax.sharding import PartitionSpec as P

F32 = jnp.float32
BF16 = jnp.bfloat16
LENGTH = 128
BASIS = 8
NEAR = 9
FAR = 1000.0
INV_CUTOFF = 0.2
CELL_SLAB = 5.0
CELL_TILE = 10.0


def silu_pair(value):
    gate = 1.0 / (1.0 + jnp.exp(-value))
    return value * gate, gate * (1.0 + value * (1.0 - gate))


OWN_SLOTS = ((0, 0), (1, 0), (2, 0))


def slots_of(flag_ref):
    flag = flag_ref[0]
    turn = (2 * flag - 1).astype(F32) * CELL_TILE
    return ((0, flag), (0, 1 - flag), (1, 1 - flag)), (turn, 0.0, -turn)


def across_lanes(rows, count):
    turned = jnp.transpose(rows)
    return [jnp.broadcast_to(turned[:, k : k + 1], (LENGTH, LENGTH)) for k in range(count)]


def stacked(rows):
    filled = sum(row.shape[0] for row in rows)
    return jnp.concatenate(rows + [jnp.zeros((LENGTH - filled, LENGTH), F32)], axis=0)


def place_atoms(pairs, slots, turns, send_ref, recv_ref):
    rows = []
    for row in range(4):
        for tile in range(3):
            ref, member = pairs[slots[tile][0]], slots[tile][1]
            cell = ref[member, row]
            real = cell[3:4] > -0.5
            shift = ((row - 1) * CELL_SLAB, turns[tile], 0.0)
            for d in range(3):
                coords = cell[d : d + 1] + shift[d]
                rows.append(jnp.where(real, coords, -FAR) * INV_CUTOFF)
                if tile == 1 and row in (1, 2):
                    recv_ref[row - 1, d : d + 1, :] = jnp.where(real, coords, FAR) * INV_CUTOFF
    for k, column in enumerate(across_lanes(stacked(rows), 36)):
        send_ref[k // 3, k % 3] = column


def folded(weights, which):
    order = lax.broadcasted_iota(jnp.int32, (BASIS, LENGTH), 0).astype(F32)
    return weights[which] * jnp.exp(-0.5 * order * (order + 1.0))


def place_weights(weights, column_ref):
    rows = stacked([folded(weights, which) for which in range(2)])
    for k, column in enumerate(across_lanes(rows, 2 * BASIS)):
        column_ref[k] = column


def banked(bank):
    return bank.at[:LENGTH], bank.at[LENGTH : 2 * LENGTH], bank.at[2 * LENGTH :]


def species_rows(embedding):
    return embedding[...].astype(F32)[:8]


def species_hot(code_row):
    order = lax.broadcasted_iota(jnp.int32, (LENGTH, LENGTH), 0)
    species = (order & 7).astype(F32)
    return jnp.where(code_row == species, 1.0, 0.0).astype(BF16)


def plain_dot(lhs, rhs, **kinds):
    return jnp.dot(lhs, rhs, preferred_element_type=F32, **kinds)


def turned_dot(lhs, rhs):
    return lax.dot_general(lhs, rhs, (((0,), (0,)), ((), ())), preferred_element_type=F32)


def pair_geometry(send_ref, recv_ref, block, cell, first, rows, hidden_from):
    apart = [
        send_ref[cell, d, pl.ds(first, rows), :] - recv_ref[block, d : d + 1, :] for d in range(3)
    ]
    square = apart[0] * apart[0] + apart[1] * apart[1] + apart[2] * apart[2]
    square = jnp.minimum(square, 1.0)
    eight = 8.0 * square
    centred = eight - 0.5
    rest = 1.0 - square
    if hidden_from is not None:
        sender = first + lax.broadcasted_iota(jnp.int32, (rows, LENGTH), 0)
        receiver = hidden_from + lax.broadcasted_iota(jnp.int32, (rows, LENGTH), 1)
        rest = jnp.where(sender == receiver, 0.0, rest)
    return apart, centred, jnp.exp(-0.5 * centred * centred), jnp.exp(eight), rest


def fill_kernels(send_ref, recv_ref, kern_ref, block):
    rows = 16

    def body(step, carry):
        first = pl.multiple_of(step * rows, rows)
        for tile in range(3):
            for near in range(3):
                own = 0 if tile == 1 and near == 1 else None
                apart, _, gauss, ratio, rest = pair_geometry(
                    send_ref, recv_ref, block, (block + near) * 3 + tile, first, rows, own
                )
                value = gauss * (rest * rest)
                narrow = [a.astype(BF16) for a in apart]
                at = pl.ds(first + (tile * 3 + near) * LENGTH, rows)
                for b in range(BASIS):
                    radial = value.astype(BF16)
                    kern_ref[at, b * LENGTH : (b + 1) * LENGTH] = radial
                    for d in range(3):
                        column = ((d + 1) * BASIS + b) * LENGTH
                        kern_ref[at, column : column + LENGTH] = radial * narrow[d]
                    if b + 1 < BASIS:
                        value = value * ratio
        return carry

    lax.fori_loop(0, LENGTH // rows, body, 0)


def weighted_sum(kern_ref, part, lhs, column_ref):
    depth = BASIS * LENGTH
    product = plain_dot(lhs, kern_ref[:, part * depth : (part + 1) * depth])
    first = min(part, 1) * BASIS
    total = product[:, :LENGTH] * column_ref[first]
    for b in range(1, BASIS):
        total = total + product[:, b * LENGTH : (b + 1) * LENGTH] * column_ref[first + b]
    return total


def nearby(pairs, slots, block, lo):
    return jnp.concatenate(
        [
            pairs[which][member, block + near, lo : lo + LENGTH, :]
            for which, member in slots
            for near in range(3)
        ],
        axis=1,
    )


def first_kernel(
    flag, even, odd, bank, weights, feat_out, hidden_out, vector_out,
    kern_ref, send_ref, recv_ref, column_ref, start_ref,
):
    mix, mixv, embedding = banked(bank)
    pairs = (even, odd)
    slots, turns = slots_of(flag)
    place_atoms(pairs, slots, turns, send_ref, recv_ref)
    place_weights(weights, column_ref)
    table = jnp.concatenate([species_rows(embedding)] * 16, axis=0).astype(BF16)
    for tile in range(3):
        for row in range(4):
            hot = species_hot(pairs[slots[tile][0]][slots[tile][1], row][3:4])
            start_ref[tile, row] = (turned_dot(table, hot) * 0.0625).astype(BF16)

    def body(block, carry):
        fill_kernels(send_ref, recv_ref, kern_ref.at[block], block)
        lhs = jnp.concatenate(
            [start_ref[tile, block + near] for tile in range(3) for near in range(3)], axis=1
        )
        invariant = weighted_sum(kern_ref.at[block], 0, lhs, column_ref)
        for d in range(3):
            vector = weighted_sum(kern_ref.at[block], d + 1, lhs, column_ref)
            vector_out[block, d] = vector
            invariant = invariant + vector * vector
            mixed = turned_dot(mixv[...], vector.astype(BF16))
            feat_out[block, (d + 1) * LENGTH : (d + 2) * LENGTH, :] = mixed.astype(BF16)
        hidden = turned_dot(mix[...], invariant.astype(BF16))
        hidden_out[block] = hidden
        start = start_ref[1, block + 1].astype(F32)
        feat_out[block, :LENGTH, :] = (start + silu_pair(hidden)[0]).astype(BF16)
        return carry

    lax.fori_loop(0, 2, body, 0)


def second_kernel(
    flag, even, feat_even, feat_mine, feat_odd, kern_ref, weights, out_weight, read, energy_out,
    pull_out, column_ref,
):
    slots, _ = slots_of(flag)
    feats = (feat_even, feat_mine, feat_odd)
    place_weights(weights, column_ref)
    mine = slots[1][1]
    (read_column,) = across_lanes(jnp.broadcast_to(read[...], (LENGTH, LENGTH)), 1)

    def body(block, carry):
        message = feat_mine[0, block + 1, :LENGTH, :].astype(F32)
        for r in range(4):
            lhs = nearby(feats, OWN_SLOTS, block, r * LENGTH)
            message = message + weighted_sum(kern_ref.at[block], r, lhs, column_ref)
        hidden = turned_dot(out_weight[...], message.astype(BF16))
        value, slope = silu_pair(hidden)
        present = even[mine, block + 1][3:4] > -0.5
        energy = jnp.sum(value * read_column, axis=0, keepdims=True)
        energy_out[block] = jnp.where(present, energy, 0.0)
        back = jnp.where(present, slope * read_column, 0.0).astype(BF16)
        pull_out[block] = plain_dot(out_weight[...], back).astype(BF16)
        return carry

    lax.fori_loop(0, 2, body, 0)


def pair_kernel(block, send_ref, recv_ref, kern_ref):
    fill_kernels(send_ref, recv_ref, kern_ref, block)


def third_kernel(
    flag, even, odd, send_ref, recv_ref, feat_even, feat_mine, feat_odd, kern_one, kern_two, pull_even, pull_mine, pull_odd,
    hidden, vectors, energies, bank, weights_one, weights_two, force_out,
    column_ref, hot_ref, feat_ref, seed_ref, deriv_even, deriv_odd,
    push_ref, own_ref,
):
    mix, mixv, embedding = banked(bank)
    pairs = (even, odd)
    feats = (feat_even, feat_mine, feat_odd)
    pulls = (pull_even, pull_mine, pull_odd)
    slots, _ = slots_of(flag)
    depth = BASIS * LENGTH
    place_weights(weights_two, column_ref)
    for tile in range(3):
        for row in range(4):
            hot_ref[row * 3 + tile] = species_hot(pairs[slots[tile][0]][slots[tile][1], row][3:4])
    push_ref[...] = jnp.zeros(push_ref.shape, F32)
    own_ref[...] = jnp.zeros(own_ref.shape, F32)
    table = species_rows(embedding)
    spreads = []
    for which in range(2):
        scale = folded(weights_one, which)
        spread = jnp.concatenate([table * scale[b : b + 1, :] for b in range(BASIS)], axis=0)
        spreads.append(spread.astype(BF16))

    def pull_back(block, kern_ref):
        lhs = nearby(pulls, OWN_SLOTS, block, 0)
        pull = pull_mine[0, block + 1].astype(F32)
        scalar_grad = pull + weighted_sum(kern_ref, 0, lhs, column_ref)
        scalar_grad = scalar_grad.astype(BF16).astype(F32)
        hidden_grad = (scalar_grad * silu_pair(hidden[block])[1]).astype(BF16)
        inv_grad = plain_dot(mix[...], hidden_grad)
        inv_grad = inv_grad.astype(BF16).astype(F32)
        grads = [inv_grad]
        for d in range(3):
            vector_grad = -weighted_sum(kern_ref, d + 1, lhs, column_ref)
            passed = plain_dot(mixv[...], vector_grad.astype(BF16))
            passed = passed.astype(BF16).astype(F32)
            grads.append(passed + 2.0 * vectors[block, d] * inv_grad)
        used = 8 * BASIS
        basis = lax.broadcasted_iota(jnp.int32, (used, LENGTH), 0) >> 3
        seed_ref[block, LENGTH + used :, :] = jnp.zeros((LENGTH - used, 4 * depth), BF16)
        for r in range(4):
            which = min(r, 1)
            table_grad = plain_dot(spreads[which], grads[r].astype(BF16))
            for b in range(BASIS):
                at = r * depth + b * LENGTH
                scaled = pull * column_ref[which * BASIS + b]
                seed_ref[block, :LENGTH, at : at + LENGTH] = scaled.astype(BF16)
                seed_ref[block, LENGTH : LENGTH + used, at : at + LENGTH] = jnp.where(
                    basis == b, table_grad, 0.0
                ).astype(BF16)

    pull_back(0, kern_one)
    pull_back(1, kern_two)
    for tile in range(3):
        for row in range(4):
            feat_ref[row * 3 + tile] = feats[tile][0, row]

    def find(pair):
        block = pair // NEAR
        place = pair - block * NEAR
        return block, place, (block + place // 3) * 3 + place % 3

    def differentiate(pair, deriv_ref):
        block, _, cell = find(pair)
        for r in range(4):
            sender = jnp.concatenate(
                [feat_ref[cell, r * LENGTH : (r + 1) * LENGTH, :], hot_ref[cell]], axis=0
            )
            deriv_ref[:, r * depth : (r + 1) * depth] = turned_dot(
                sender, seed_ref[block, :, r * depth : (r + 1) * depth]
            )

    def chain(pair, deriv_ref):
        sums = [jnp.zeros((16, LENGTH), F32)] * 3
        block, place, cell = find(pair)
        hidden_from = jnp.where(place == 4, 0, 4 * LENGTH)
        rows = 16
        for step in range(LENGTH // rows):
            first = step * rows
            apart, centred, gauss, ratio, rest = pair_geometry(
                send_ref, recv_ref, block, cell, first, rows, hidden_from
            )
            along = [None, None, None]
            value = None
            slope = None
            for b in range(BASIS - 1, -1, -1):
                parts = []
                for r in range(4):
                    at = r * depth + b * LENGTH
                    parts.append(deriv_ref[first : first + rows, at : at + LENGTH])
                joint = parts[0]
                for d in range(3):
                    part = parts[d + 1]
                    joint = joint + apart[d] * part
                    along[d] = part if along[d] is None else along[d] * ratio + part
                if value is None:
                    value = joint
                else:
                    slope = value if slope is None else slope * ratio + value
                    value = value * ratio + joint
            slope = slope * ratio
            scale = gauss * rest
            radial = scale * (8.0 * rest * (slope - centred * value) - 2.0 * value)
            radial = radial * (2.0 * INV_CUTOFF)
            envelope = scale * rest * INV_CUTOFF
            for d in range(3):
                pushed = envelope * along[d] + radial * apart[d]
                push_ref[cell, d, first : first + rows, :] += pushed
                sums[d] = sums[d] + pushed
        for d in range(3):
            own_ref[block, d] += sums[d]

    differentiate(0, deriv_even)

    def pair_steps(step, carry):
        pair = step * 2
        differentiate(pair + 1, deriv_odd)
        chain(pair, deriv_even)
        differentiate(jnp.minimum(pair + 2, 2 * NEAR - 1), deriv_even)
        chain(pair + 1, deriv_odd)
        return carry

    lax.fori_loop(0, NEAR, pair_steps, 0)
    force_out[...] = jnp.zeros(force_out.shape, F32)
    ones = jnp.ones((16, 2 * LENGTH), BF16)
    for row in range(4):
        for tile in range(3):
            for d in range(3):
                total = push_ref[row * 3 + tile, d]
                high = total.astype(BF16)
                low = (total - high.astype(F32)).astype(BF16)
                parts = jnp.concatenate([high, low], axis=1)
                pushed = lax.dot_general(
                    ones, parts, (((1,), (1,)), ((), ())), preferred_element_type=F32
                )[:1]
                if tile == 1 and row in (1, 2):
                    pushed = pushed - jnp.sum(own_ref[row - 1, d], axis=0, keepdims=True)
                force_out[tile, row, d : d + 1, :] = -pushed
    for block in range(2):
        force_out[1, block + 1, 3:4, :] = energies[block]


AXES = ("slab", "tile")


class Grid:
    def __init__(self, slabs, tiles):
        self.slabs, self.tiles = slabs, tiles
        self.moved = (slabs, tiles) == (16, 32)
        self.cycle = [(0, 0), (0, 1), (0, 2), (0, 3), (1, 3), (1, 2), (1, 1), (2, 1)]
        self.cycle += [(2, 2), (2, 3), (3, 3), (3, 2), (3, 1), (3, 0), (2, 0), (1, 0)]

    def device(self, slab, tile):
        slab, tile = slab % self.slabs, tile % self.tiles
        if self.moved:
            x, y = self.cycle[slab]
            z, core = tile // 2, (tile // 2 + tile) % 2
            slab, tile = x * 4 + z % 4, ((z // 4) * 4 + y) * 2 + core
        return slab * self.tiles + tile

    def places(self):
        return [(slab, tile) for slab in range(self.slabs) for tile in range(self.tiles)]

    def flag(self):
        odd = lax.axis_index("tile")
        if self.moved:
            odd = odd + lax.axis_index("slab")
        return (1 - odd % 2).astype(jnp.int32)

    def to_work(self, block):
        if not self.moved:
            return block
        route = [(s * self.tiles + t, self.device(s, t)) for s, t in self.places()]
        return lax.ppermute(block, AXES, route)

    def to_owner(self, block):
        if not self.moved:
            return block
        route = [(self.device(s, t), s * self.tiles + t) for s, t in self.places()]
        return lax.ppermute(block, AXES, route)

    def along_slab(self, block, step):
        route = [(self.device(s, t), self.device(s + step, t)) for s, t in self.places()]
        return lax.ppermute(block, AXES, route)

    def with_partner(self, block, odd):
        groups = [
            [self.device(s, t + odd), self.device(s, t + odd + 1)]
            for s, t in self.places()
            if t % 2 == 0
        ]
        return lax.all_gather(block, AXES, axis_index_groups=groups)

    def swap(self, block, odd):
        route = []
        for s, t in self.places():
            if t % 2 == 0:
                ends = self.device(s, t + odd), self.device(s, t + odd + 1)
                route += [ends, ends[::-1]]
        return lax.ppermute(block, AXES, route)

    def column(self, cells):
        above = self.along_slab(cells[1:], 1)
        below = self.along_slab(cells[:1], -1)
        return jnp.concatenate([above, cells, below], axis=0)

    def gather_near(self, cells):
        column = self.column(cells)
        return self.with_partner(column, 0), self.with_partner(column, 1)

    def swap_near(self, cells):
        column = self.column(cells)[None]
        return self.swap(column, 0), column, self.swap(column, 1)

    def send_home(self, parts, flag):
        even = self.with_partner(parts[0], 0)
        odd = self.with_partner(parts[2], 1)
        column = (
            parts[1]
            + lax.dynamic_index_in_dim(even, flag, 0, False)
            + lax.dynamic_index_in_dim(odd, 1 - flag, 0, False)
        )
        from_next = self.along_slab(column[:1], -1)
        from_last = self.along_slab(column[3:], 1)
        return column[1:3] + jnp.concatenate([from_last, from_next], axis=0)


def kernel_call(body, outs, scratch, flops, operands, room, flagged=True):
    in_specs = [pl.BlockSpec(memory_space=pltpu.VMEM)] * operands
    if flagged:
        in_specs[0] = pl.BlockSpec(memory_space=pltpu.SMEM)
    return pl.pallas_call(
        body,
        out_shape=[jax.ShapeDtypeStruct(shape, kind) for shape, kind in outs],
        in_specs=in_specs,
        out_specs=[pl.BlockSpec(memory_space=pltpu.VMEM)] * len(outs),
        scratch_shapes=[pltpu.VMEM(shape, kind) for shape, kind in scratch],
        compiler_params=pltpu.CompilerParams(vmem_limit_bytes=room * 1024 * 1024),
        cost_estimate=pl.CostEstimate(flops=flops, bytes_accessed=1 << 20, transcendentals=0),
    )


GEOMETRY = [
    ((12, 3, LENGTH, LENGTH), F32),
    ((2, 3, LENGTH), F32),
    ((2 * BASIS, LENGTH, LENGTH), F32),
]


def first_call():
    outs = [
        ((2, 4 * LENGTH, LENGTH), BF16),
        ((2, LENGTH, LENGTH), F32),
        ((2, 3, LENGTH, LENGTH), F32),
        ((2, NEAR * LENGTH, 4 * BASIS * LENGTH), BF16),
        ((12, 3, LENGTH, LENGTH), F32),
        ((2, 3, LENGTH), F32),
    ]
    scratch = GEOMETRY[2:] + [((3, 4, LENGTH, LENGTH), BF16)]
    return kernel_call(first_kernel, outs, scratch, 2400000000, 5, 18)


def second_call():
    outs = [((2, 1, LENGTH), F32), ((2, LENGTH, LENGTH), BF16)]
    return kernel_call(second_kernel, outs, GEOMETRY[2:], 2400000000, 9, 18)


def pair_call(block):
    outs = [((NEAR * LENGTH, 4 * BASIS * LENGTH), BF16)]
    body = functools.partial(pair_kernel, block)
    return kernel_call(body, outs, [], 900000000, 2, 18, False)


def third_call():
    scratch = GEOMETRY[2:] + [
        ((12, LENGTH, LENGTH), BF16),
        ((12, 4 * LENGTH, LENGTH), BF16),
        ((2, 2 * LENGTH, 4 * BASIS * LENGTH), BF16),
        ((LENGTH, 4 * BASIS * LENGTH), F32),
        ((LENGTH, 4 * BASIS * LENGTH), F32),
        ((12, 3, LENGTH, LENGTH), F32),
        ((2, 3, 16, LENGTH), F32),
    ]
    return kernel_call(third_kernel, [((3, 4, 4, LENGTH), F32)], scratch, 7200000000, 19, 18)


def on_device(
    grid, positions, species, occupied, embedding, first_radial_weight, radial_two, mix_scalar,
    vector_channel_weight, out_weight, read_weight,
):
    codes = jnp.where(occupied > 0, species, -1).astype(F32)
    packet = jnp.concatenate([positions, codes[:, :, None]], axis=2)[:, 0]
    flag = grid.flag()
    spare = jnp.zeros((16 - embedding.shape[0], LENGTH), BF16)
    bank = jnp.concatenate([mix_scalar, vector_channel_weight, embedding, spare], axis=0)
    weights_one = first_radial_weight * 0.25
    weights_two = radial_two * 0.25
    places = (flag[None], *grid.gather_near(grid.to_work(packet)))
    features, hidden, vectors, kernels, senders, receivers = first_call()(
        *places, bank, weights_one
    )
    near_features = grid.swap_near(features)
    energies, pull = second_call()(
        *places[:2], *near_features, kernels, weights_two, out_weight, read_weight[None, :]
    )
    pull, senders, receivers = lax.optimization_barrier((pull, senders, receivers))
    near_pulls = grid.swap_near(pull)
    again = [pair_call(block)(senders, receivers)[0] for block in range(2)]
    (parts,) = third_call()(
        *places, senders, receivers, *near_features, *again, *near_pulls, hidden, vectors, energies, bank,
        weights_one, weights_two,
    )
    final = grid.to_owner(grid.send_home(parts, flag))
    return final[:, 3:], final[:, None, :3]


def solution(mesh):
    grid = Grid(mesh.shape["slab"], mesh.shape["tile"])
    in_specs = (
        P("slab", "tile", None, None),
        P("slab", "tile", None),
        P("slab", "tile", None),
        P(),
        P(),
        P(),
        P(),
        P(),
        P(),
        P(),
    )
    out_specs = (P("slab", "tile", None), P("slab", "tile", None, None))
    return jax.shard_map(
        functools.partial(on_device, grid), mesh=mesh, in_specs=in_specs, out_specs=out_specs, check_vma=False
    )
```
